32 devices in a mesh: seq: 8 (over z, x), head: 4 (over y, core).
Axes of the slice: x: 2, y: 2, z: 4, core: 2. Of those that a mesh axis runs over, the one named last changes fastest.
Arguments:
- tokens: bfloat16 [64, 1024, 768], P('seq', 'head'), may hold values from -1.1953125 to 1.1953125
- cotangent: bfloat16 [64, 1024, 768], P('seq', 'head'), may hold values from -6 to 6
- lengths: int32 [64], P('seq'), may hold values from 0 to 1024, as said below
- owners: int32 [64], P('seq'), may hold values from 0 to 7, as said below
- codons: int32 [64, 1024], P('seq'), may hold values from 0 to 63
- ln1_gain: bfloat16 [768], P('head'), may hold values from 0.5 to 1.5
- ln1_bias: bfloat16 [768], P('head'), may hold values from -1.75 to 1.75
- w_query: bfloat16 [768, 768], P('head'), may hold values from -0.21875 to 0.21875
- b_query: bfloat16 [768], P('head'), may hold values from -1.75 to 1.75
- w_key: bfloat16 [768, 768], P('head'), may hold values from -0.21875 to 0.21875
- b_key: bfloat16 [768], P('head'), may hold values from -1.75 to 1.75
- w_value: bfloat16 [768, 768], P('head'), may hold values from -0.21875 to 0.21875
- b_value: bfloat16 [768], P('head'), may hold values from -1.75 to 1.75
- w_out: bfloat16 [768, 768], P('head'), may hold values from -0.3125 to 0.3125
- b_out: bfloat16 [768], P('head'), may hold values from -1.75 to 1.75
- ln2_gain: bfloat16 [768], P('head'), may hold values from 0.5 to 1.5
- ln2_bias: bfloat16 [768], P('head'), may hold values from -1.75 to 1.75
- w_up: bfloat16 [768, 3072], P(None, 'head'), may hold values from -0.5 to 0.5
- b_up: bfloat16 [3072], P('head'), may hold values from -1.75 to 1.75
- w_down: bfloat16 [3072, 768], P('head'), may hold values from -0.3125 to 0.3125
- b_down: bfloat16 [768], P('head'), may hold values from -1.75 to 1.75
Outputs:
- mixed: bfloat16 [64, 1024, 768], P('seq', 'head')
- input_grad: bfloat16 [64, 1024, 768], P('seq', 'head')
- grad_ln1_gain: float32 [768], P('head')
- grad_ln1_bias: float32 [768], P('head')
- grad_w_query: float32 [768, 768], P('head')
- grad_b_query: float32 [768], P('head')
- grad_w_key: float32 [768, 768], P('head')
- grad_b_key: float32 [768], P('head')
- grad_w_value: float32 [768, 768], P('head')
- grad_b_value: float32 [768], P('head')
- grad_w_out: float32 [768, 768], P('head')
- grad_b_out: float32 [768], P('head')
- second_layer_norm_gain_gradient: float32 [768], P('head')
- grad_ln2_bias: float32 [768], P('head')
- grad_w_up: float32 [768, 3072], P(None, 'head')
- grad_b_up: float32 [3072], P('head')
- grad_w_down: float32 [3072, 768], P('head')
- grad_b_down: float32 [768], P('head')
- histogram: int32 [8, 64], P('seq')
The draws below stay inside these ranges and needn't reach their ends.
Inputs may be any that keep to these rules, and one draw needn't show every extreme that they name: `lengths`: A device's sequences of nonzero length stand in its first slots and empty slots have length 0; on the first device of each group of 8 all 8 slots hold a sequence, and some sequence has 1024 codons. The sequences of nonzero length on one device go to distinct owners whose index // 8 equals the device's index // 8, and every owner receives exactly 4 of them.
All inputs are finite; a program needn't handle non-finite values.
Results may differ from the reference program's by a relative error of at most 0.015.
Values may be sent and summed in bfloat16 or wider, within the bound.
No kernel may reach another device: no remote copies, remote signals or barrier semaphores. Data moves between devices by JAX's collectives and lax.ppermute only.
A program may use at most 320 MiB of HBM per device.

```python
import jax
import jax.numpy as jnp
from jax import lax

D = 768
NH = 12
HD = 64
FF = 3072
CODONS = 64
LMAX = 1024
LMIN = 100
GROUP = 8
SEQ_DEV = 4
SLOTS = 8
BUCKETS = 8
SLOTS_ALL = 64
N_SEQ = 8


def bucket_plan(key):
    groups = N_SEQ // GROUP
    keys_all = jax.random.split(key, 4)
    ranked = jnp.tile(jnp.arange(GROUP, dtype=jnp.int32)[None, :], (groups, 1))
    order = jax.random.permutation(keys_all[0], ranked, axis=1, independent=True)
    placed = jax.random.permutation(keys_all[1], ranked, axis=1, independent=True)
    lifted = jax.random.randint(keys_all[2], (groups, GROUP // 2), 0, SEQ_DEV + 1)
    fullest = jax.random.randint(keys_all[3], (groups, 1), 0, GROUP // 2)
    lifted = jnp.where(jnp.arange(GROUP // 2)[None, :] == fullest, SEQ_DEV, lifted)
    target_place = 2 * fullest
    first_place = placed[:, 0:1]
    column_number = jnp.arange(GROUP)[None, :]
    placed = jnp.where(placed == target_place, first_place, placed)
    placed = jnp.where(column_number == 0, target_place, placed)
    counts = jnp.stack([SEQ_DEV + lifted, SEQ_DEV - lifted], axis=2).reshape(groups, GROUP)
    starts = jnp.cumsum(counts, axis=1) - counts
    source = jnp.arange(SLOTS_ALL) // SLOTS
    within = jnp.arange(SLOTS_ALL) % SLOTS
    group_of = source // GROUP
    cycle_place = placed[group_of, source % GROUP]
    owner = group_of * GROUP + order[group_of, (starts[group_of, cycle_place] + within) % GROUP]
    living = within < counts[group_of, cycle_place]
    topmost = (cycle_place == 2 * fullest[group_of, 0]) & (within == 0)
    return (owner.astype(jnp.int32), living, topmost)


def draw_owners(key, part):
    owner, living, topmost = bucket_plan(key)
    return owner


def draw_lengths(key, part):
    owner, living, topmost = bucket_plan(key)
    key = jax.random.fold_in(key, 7)
    first_key, second_key = jax.random.split(key)
    shifts = jax.random.randint(first_key, (BUCKETS,), 0, 5)
    reach = jnp.right_shift(jnp.full((SLOTS_ALL,), LMAX - LMIN + 1, jnp.int32), shifts[owner])
    reach = jnp.maximum(reach, 1)
    dropped = jax.random.randint(second_key, (SLOTS_ALL,), 0, reach)
    sizes_drawn = jnp.where(topmost, LMAX, LMAX - dropped)
    return jnp.where(living, sizes_drawn, 0).astype(jnp.int32)


def touch_ends(values, stream_key, low, top_value):
    spot = [jax.random.randint(jax.random.fold_in(stream_key, axis), (), 0, length) for axis, length in enumerate(values.shape)]
    widest = values.shape.index(max(values.shape))
    next_to = spot[:widest] + [(spot[widest] + 1) % values.shape[widest]] + spot[widest + 1:]
    return values.at[tuple(spot)].set(low).at[tuple(next_to)].set(top_value)


def level_of(key, dims, cuts, low, top_value):
    level = 1.0
    for position, blocks in cuts:
        steps = jax.random.uniform(jax.random.fold_in(jax.random.fold_in(key, 6), position), (blocks,), jnp.float32, low / len(cuts), top_value / len(cuts))
        level = level * jnp.repeat(jnp.exp(steps), dims[position] // blocks).reshape((-1,) + (1,) * (len(dims) - 1 - position))
    return level


def normal_values(own_key, extent, scale, most, cuts=(), kind=jnp.bfloat16):
    values = scale * jax.random.normal(own_key, extent, jnp.float32)
    if cuts:
        values = values * level_of(own_key, extent, cuts, -0.22, 0.18)
    return jnp.clip(values, -most, most).astype(kind)


def setup_inputs(seed: int = 0) -> dict:
    key_list = jax.random.split(jax.random.key(seed), 22)
    return {
        "tokens": normal_values(key_list[0], (SLOTS_ALL, LMAX, D), 0.2, 1.1953125, ((0, 8), (1, 4))),
        "cotangent": normal_values(key_list[1], (SLOTS_ALL, LMAX, D), 1.0, 6.0, ((0, 8), (1, 4))),
        "lengths": draw_lengths(jax.random.fold_in(key_list[21], 71), 0),
        "owners": draw_owners(jax.random.fold_in(key_list[21], 71), 0),
        "codons": touch_ends(jax.random.randint(key_list[4], (SLOTS_ALL, LMAX), 0, CODONS), jax.random.fold_in(key_list[4], 1), 0, CODONS - 1).astype(jnp.int32),
        "ln1_gain": jnp.clip(1.0 + 0.1 * jax.random.normal(key_list[5], (D,), jnp.float32), 0.5, 1.5).astype(jnp.bfloat16),
        "ln1_bias": normal_values(key_list[6], (D,), 0.3, 1.75, ((0, 4),)),
        "w_query": normal_values(key_list[7], (D, D), D ** -0.5, 0.21875, ((0, 4),)),
        "b_query": normal_values(key_list[8], (D,), 0.3, 1.75, ((0, 4),)),
        "w_key": normal_values(key_list[9], (D, D), D ** -0.5, 0.21875, ((0, 4),)),
        "b_key": normal_values(key_list[10], (D,), 0.3, 1.75, ((0, 4),)),
        "w_value": normal_values(key_list[11], (D, D), D ** -0.5, 0.21875, ((0, 4),)),
        "b_value": normal_values(key_list[12], (D,), 0.3, 1.75, ((0, 4),)),
        "w_out": normal_values(key_list[13], (D, D), (D // 2) ** -0.5, 0.3125, ((0, 4),)),
        "b_out": normal_values(key_list[14], (D,), 0.3, 1.75, ((0, 4),)),
        "ln2_gain": jnp.clip(1.0 + 0.1 * jax.random.normal(key_list[15], (D,), jnp.float32), 0.5, 1.5).astype(jnp.bfloat16),
        "ln2_bias": normal_values(key_list[16], (D,), 0.3, 1.75, ((0, 4),)),
        "w_up": normal_values(key_list[17], (D, FF), (D // 5) ** -0.5, 0.5, ((1, 4),)),
        "b_up": normal_values(key_list[18], (FF,), 0.3, 1.75, ((0, 4),)),
        "w_down": normal_values(key_list[19], (FF, D), (FF // 8) ** -0.5, 0.3125, ((0, 4),)),
        "b_down": normal_values(key_list[20], (D,), 0.3, 1.75, ((0, 4),)),
    }


@jax.custom_vjp
def low(v):
    return lax.optimization_barrier(v.astype(jnp.bfloat16)).astype(jnp.float32)

@jax.custom_vjp
def low_back(v):
    return v

def low_keep(v):
    return (low(v), None)

def low_pass(kept, grad):
    return (grad,)

def back_keep(v):
    return (v, None)

def back_low(kept, grad):
    return (low(grad),)
low.defvjp(low_keep, low_pass)
low_back.defvjp(back_keep, back_low)
EPSILON = 1e-05
NEGATIVE = -1e+30
HIGHEST = lax.Precision.HIGHEST

def layer_norm(values, gain, offset):
    center = lax.optimization_barrier(jnp.mean(values, axis=-1, keepdims=True))
    shifted = values - center
    spread = lax.optimization_barrier(jnp.mean(shifted * shifted, axis=-1, keepdims=True))
    return shifted * lax.rsqrt(spread + EPSILON) * gain + offset

def rotary_tables(sequence_length, size):
    half_size = size // 2
    frequency = 10000.0 ** (-(jnp.arange(half_size, dtype=jnp.float32) * 2.0 / size))
    angles = jnp.arange(sequence_length, dtype=jnp.float32)[:, None] * frequency[None, :]
    return (jnp.cos(angles), jnp.sin(angles))

def rotate(values, cos_table, sin_table):
    half_size = values.shape[-1] // 2
    former = values[..., :half_size]
    latter = values[..., half_size:]
    cos_part = cos_table[:, None, :]
    sin_part = sin_table[:, None, :]
    return jnp.concatenate([former * cos_part - latter * sin_part, latter * cos_part + former * sin_part], axis=-1)

def block_forward(params, block_rows, block_lengths):
    first_norm_gain, first_norm_bias, w_query, b_query, w_key, b_key, w_value, b_value, w_out, b_out, second_norm_gain, second_norm_bias, w_up, b_up, w_down, b_down = params
    slot_count = block_rows.shape[0]
    scale_factor = HD ** (-0.5)
    flat_rows = block_rows.reshape(slot_count * LMAX, D)
    normed = low(layer_norm(flat_rows, first_norm_gain, first_norm_bias))
    cos_table, sin_table = rotary_tables(LMAX, HD)
    query_pre = low_back(jnp.dot(normed, w_query.T, precision=HIGHEST)) + b_query
    key_pre = low_back(jnp.dot(normed, w_key.T, precision=HIGHEST)) + b_key
    queries = low(rotate(query_pre.reshape(slot_count, LMAX, NH, HD), cos_table, sin_table))
    key_rot = low(rotate(key_pre.reshape(slot_count, LMAX, NH, HD), cos_table, sin_table))
    values = low(low_back(jnp.dot(normed, w_value.T, precision=HIGHEST)) + b_value).reshape(slot_count, LMAX, NH, HD)
    live_keys = jnp.arange(LMAX)[None, :] < block_lengths[:, None]
    scores = low_back(jnp.einsum('bqhd,bkhd->bhqk', queries, key_rot, precision=HIGHEST) * scale_factor)
    scores = jnp.where(live_keys[:, None, None, :], scores, NEGATIVE)
    weights = jax.nn.softmax(scores, axis=-1)
    context = jnp.einsum('bhqk,bkhd->bqhd', low(weights), values, precision=HIGHEST)
    context = low(low_back(context.reshape(slot_count * LMAX, D)))
    middle = flat_rows + low_back(jnp.dot(context, w_out, precision=HIGHEST)) + b_out
    second_normalized_rows = low(layer_norm(middle, second_norm_gain, second_norm_bias))
    hidden_pre = low_back(jnp.dot(second_normalized_rows, w_up, precision=HIGHEST)) + b_up
    hidden = low(jax.nn.gelu(hidden_pre, approximate=False))
    result = middle + low_back(jnp.dot(hidden, w_down, precision=HIGHEST)) + b_down
    keep_rows = live_keys.reshape(slot_count * LMAX, 1)
    return jnp.where(keep_rows, result, 0.0).reshape(slot_count, LMAX, D)

def forward(params, tokens_all, lengths):
    group_size = 4 if SLOTS_ALL % 4 == 0 else 1
    blocks = SLOTS_ALL // group_size
    grouped = tokens_all.reshape(blocks, group_size, LMAX, D)
    grouped_lengths = lengths.reshape(blocks, group_size)
    checked = jax.checkpoint(block_forward)

    def one_block(running, pieces):
        return (running, checked(params, pieces[0], pieces[1]))
    _, outputs = lax.scan(one_block, jnp.zeros((), jnp.float32), (grouped, grouped_lengths))
    return outputs.reshape(SLOTS_ALL, LMAX, D)

def count_codons(lengths, owners, codons):
    live_rows = jnp.arange(LMAX)[None, :] < lengths[:, None]
    codon_index = jnp.arange(CODONS)
    matches = (codons[:, :, None] == codon_index[None, None, :]) & live_rows[:, :, None]
    per_sequence = lax.optimization_barrier(jnp.sum(matches.astype(jnp.int32), axis=1)).astype(jnp.int32)
    owner_match = (owners[:, None] == jnp.arange(BUCKETS)[None, :]).astype(jnp.int32)
    return lax.optimization_barrier(jnp.sum(owner_match[:, :, None] * per_sequence[:, None, :], axis=0)).astype(jnp.int32)

def reference(tokens, cotangent, lengths, owners, codons, ln1_gain, ln1_bias, w_query, b_query, w_key, b_key, w_value, b_value, w_out, b_out, ln2_gain, ln2_bias, w_up, b_up, w_down, b_down):
    params = tuple((weight.astype(jnp.float32) for weight in (ln1_gain, ln1_bias, w_query, b_query, w_key, b_key, w_value, b_value, w_out, b_out, ln2_gain, ln2_bias, w_up, b_up, w_down, b_down)))
    outputs, pullback = jax.vjp(lambda weights, inputs: forward(weights, inputs, lengths), params, tokens.astype(jnp.float32))
    gradients, input_grad = pullback(cotangent.astype(jnp.float32))
    histogram = count_codons(lengths, owners, codons)
    return (outputs.astype(jnp.bfloat16), input_grad.astype(jnp.bfloat16), gradients[0], gradients[1], gradients[2], gradients[3], gradients[4], gradients[5], gradients[6], gradients[7], gradients[8], gradients[9], gradients[10], gradients[11], gradients[12], gradients[13], gradients[14], gradients[15], histogram)
```

```python
import functools
import math

import jax
import jax.numpy as jnp
from jax import lax
from jax.experimental import pallas as pl
from jax.experimental.pallas import tpu as pltpu
from jax.sharding import PartitionSpec as P

HD = 64
CODONS = 64
EPSILON = 1e-05
NEGATIVE = -1e30
PAIR = 2 * HD
LOG2E = 1.4426950408889634
QUERY_SCALE = HD ** (-0.5) * LOG2E
QCHUNK = 256
KCHUNK = 512
FCHUNK = 256
STRIP = 128
CALLS = ((0, 1), (1, 2), (3, 1), (4, 1), (5, 1))
PART_BITS = 2
PARTS = 1 << PART_BITS
UNIT = 16
VECTOR_ROWS = 16
SMALL_ROWS = 16

F32 = jnp.float32
BF16 = jnp.bfloat16
MIB = 1024 * 1024
LIMIT = 60 * MIB


def dot_nn(a, b):
    return lax.dot_general(a, b, (((1,), (0,)), ((), ())), preferred_element_type=F32)


def dot_nt(a, b):
    return lax.dot_general(a, b, (((1,), (1,)), ((), ())), preferred_element_type=F32)


def standardize(rows):
    center = jnp.mean(rows, axis=-1, keepdims=True)
    shifted = rows - center
    inverse = lax.rsqrt(jnp.mean(shifted * shifted, axis=-1, keepdims=True) + EPSILON)
    return shifted * inverse, inverse


def turn(tile, cos, sin):
    lane = lax.broadcasted_iota(jnp.int32, tile.shape, 1)
    swapped = jnp.where(
        lane % HD < HD // 2,
        pltpu.roll(tile, PAIR - HD // 2, 1),
        pltpu.roll(tile, HD // 2, 1),
    )
    return tile * cos + swapped * sin


def split_three(value):
    high = value.astype(BF16).astype(F32)
    rest = value - high
    mid = rest.astype(BF16).astype(F32)
    return high, mid, rest - mid


def aligned(value, multiple):
    return pl.multiple_of(value, multiple)


class RowCopy:
    def __init__(self, piece, target, sems):
        slots, portion, _ = target.shape
        self.copies = [
            pltpu.make_async_copy(
                piece.at[pl.ds(n * portion, portion)], target.at[n], sems.at[n]
            )
            for n in range(slots)
        ]

    def start(self):
        for copy in self.copies:
            copy.start()

    def wait(self):
        for copy in self.copies:
            copy.wait()


def fetch(step, pieces, buffer, sems):
    copies = [
        RowCopy(pieces[k], buffer.at[k % 2], sems.at[k % 2]) for k in range(len(pieces))
    ]

    @pl.when(step == 0)
    def _():
        copies[0].start()

    for k, copy in enumerate(copies):
        @pl.when(step == k - 1)
        def _(copy=copy):
            copy.start()

    for k, copy in enumerate(copies):
        @pl.when(step == k)
        def _(copy=copy):
            copy.wait()


def emit(step, value, targets, buffer, sems):
    copies = [
        pltpu.make_async_copy(buffer.at[k % 2], targets[k], sems.at[k % 2])
        for k in range(len(targets))
    ]
    last = len(copies) - 1
    for k in range(2, len(copies)):
        @pl.when(step == k)
        def _(k=k):
            copies[k - 2].wait()

    buffer[step % 2] = value
    for k, copy in enumerate(copies):
        @pl.when(step == k)
        def _(copy=copy):
            copy.start()

    @pl.when(step == last)
    def _():
        for copy in copies[max(last - 1, 0) :]:
            copy.wait()


def weight_plan(meta, rows):
    here, side = meta[0], meta[1] % 2
    half = rows // 2
    return [
        (0, here, 0, rows),
        (1, here ^ 1, 0, rows),
        (2, here ^ 2, side * half, half),
        (3, here ^ 2, (1 - side) * half, half),
        (4, here ^ 3, side * half, half),
        (5, here ^ 3, (1 - side) * half, half),
    ]


def head_copies(meta, pieces, which, target, sems, base):
    copies = []
    for i, block, offset, size in weight_plan(meta, HEADS_EACH * HD):
        step = size // HEADS_EACH
        for c in range(HEADS_EACH):
            row = offset + c * step
            place = (row // HD * HEAD_DEVICES + block) * HD + row % HD
            copies.append(
                pltpu.make_async_copy(
                    pieces[i].at[pl.ds(SQUARE_FIRST[i] + which * size + c * step, step)],
                    target.at[pl.ds(aligned(place, UNIT), step)],
                    sems.at[base + len(copies)],
                )
            )
    return copies


def block_copies(meta, pieces, which, target, sems, base):
    return [
        pltpu.make_async_copy(
            pieces[i].at[which],
            target.at[block, pl.ds(aligned(offset, UNIT), size)],
            sems.at[base + i],
        )
        for i, block, offset, size in weight_plan(meta, pieces[0].shape[1])
    ]


HEADS_EACH = 3
HEAD_DEVICES = 4
SQUARE_FIRST = (0, 0, 512, 0, 0, 0)
PIECES = 6
HEAD_COPIES = PIECES * HEADS_EACH


def project_kernel(count, meta, *refs):
    toks, weights = refs[:count], refs[count : count + PIECES]
    vec, cos_ref, sin_ref = refs[count + PIECES : count + PIECES + 3]
    n_out, q_out, k_out, v_out, buffer, wq, wk, wv, tok_sems, sems = refs[count + PIECES + 3 :]
    step = pl.program_id(0)
    _, slots, portion, width = buffer.shape
    copies = []
    for i, ref in enumerate((wq, wk, wv)):
        copies += head_copies(meta, weights, i, ref, sems, i * HEAD_COPIES)

    @pl.when(step == 0)
    def _():
        for copy in copies:
            copy.start()

    fetch(step, toks, buffer, tok_sems)
    tok = buffer[step % 2].reshape(slots * portion, width).astype(F32)
    standard, _ = standardize(tok)
    normed = (standard * vec[5:6, :] + vec[6:7, :]).astype(BF16)
    n_out[...] = normed.reshape(slots, portion, width)

    @pl.when(step == 0)
    def _():
        for copy in copies:
            copy.wait()

    cos = jnp.concatenate([cos_ref[...]] * slots, axis=0)
    sin = jnp.concatenate([sin_ref[...]] * slots, axis=0)
    query = dot_nt(normed, wq[...]) + vec[0:1, :]
    key = dot_nt(normed, wk[...]) + vec[1:2, :]
    for j in range(width // PAIR):
        at = slice(j * PAIR, (j + 1) * PAIR)
        q_out[:, :, at] = (
            (turn(query[:, at], cos, sin) * QUERY_SCALE)
            .astype(BF16)
            .reshape(slots, portion, PAIR)
        )
        k_out[:, :, at] = (
            turn(key[:, at], cos, sin).astype(BF16).reshape(slots, portion, PAIR)
        )
    value = dot_nt(normed, wv[...]) + vec[2:3, :]
    v_out[...] = value.astype(BF16).reshape(slots, portion, width)


def attend_kernel(slot, meta, q_ref, k_ref, v_ref, *refs):
    o_ref, rest_ref, st_ref = refs[-3:]
    length = meta[2 + slot]
    rows = k_ref.shape[1]
    lane = lax.broadcasted_iota(jnp.int32, (rows, PAIR), 1)
    place_in = lax.broadcasted_iota(jnp.int32, (rows, PAIR), 0)
    halves = [(lane // HD == h).astype(F32).astype(BF16) for h in range(2)]
    guard = jnp.where(
        lane % HD == 3, jnp.where(place_in < length, 0.0, NEGATIVE), 1.0
    ).astype(BF16)
    keys = jnp.concatenate([k_ref[0], guard], axis=1)
    values = v_ref[0]
    values_h = [values * half + (1.0 - half) for half in halves]
    short = (QCHUNK, PAIR)
    lane_c = lax.broadcasted_iota(jnp.int32, short, 1)
    first = lane_c < HD
    within = lane_c % HD
    flag = (lane_c == 3).astype(F32).astype(BF16)

    def scores_of(i):
        c, h = divmod(i, 2)
        at = slice(c * QCHUNK, (c + 1) * QCHUNK)
        query = jnp.concatenate([q_ref[0, at, :] * halves[h][:QCHUNK], flag], axis=1)
        return dot_nt(query, keys)

    steps = 2 * (rows // QCHUNK)
    following = scores_of(0)
    outs, logs = [], []
    for i in range(steps):
        c, h = divmod(i, 2)
        scores = following
        if i + 1 < steps:
            following = scores_of(i + 1)
        top = jnp.max(scores, axis=1, keepdims=True)
        weights = jnp.exp2(scores - top).astype(BF16)
        sums = dot_nn(weights, values_h[h])
        total = pltpu.roll(sums, HD, 1)
        outs.append(sums / total)
        logs.append(-top - jnp.log(total) * LOG2E)
        if h == 1:
            at = slice(c * QCHUNK, (c + 1) * QCHUNK)
            context = jnp.where(first, outs[0], outs[1])
            o_ref[0, at, :] = context.astype(BF16)
            rest_ref[0, at, :] = (context - context.astype(BF16).astype(F32)).astype(BF16)
            high, mid, low = split_three(jnp.where(first, logs[0], logs[1]))
            st_ref[0, at, :] = jnp.where(
                within == 0,
                high,
                jnp.where(
                    within == 1,
                    mid,
                    jnp.where(within == 2, low, jnp.where(within == 3, 1.0, 0.0)),
                ),
            ).astype(BF16)
            outs, logs = [], []


def attend_back_kernel(
    meta,
    q_ref,
    k_ref,
    v_ref,
    do_ref,
    o_ref,
    rest_ref,
    st_ref,
    cos_ref,
    sin_ref,
    dq_ref,
    dk_ref,
    dv_ref,
    sums_ref,
    dqt,
):
    length = meta[2 + pl.program_id(0)]
    rows = k_ref.shape[1]
    lane = lax.broadcasted_iota(jnp.int32, (rows, PAIR), 1)
    within = lane % HD
    place_in = lax.broadcasted_iota(jnp.int32, (rows, PAIR), 0)
    halves = [(lane // HD == h).astype(F32).astype(BF16) for h in range(2)]
    guard = jnp.where(within == 3, jnp.where(place_in < length, 0.0, NEGATIVE), 1.0).astype(BF16)
    key = k_ref[0]
    keys = jnp.concatenate([key, guard], axis=1)
    values = jnp.concatenate([v_ref[0], jnp.ones((rows, PAIR), BF16)], axis=1)
    grads = do_ref[0]
    product = grads.astype(F32) * (o_ref[0].astype(F32) + rest_ref[0].astype(F32))
    p_high = product.astype(BF16)
    p_low = (product - p_high.astype(F32)).astype(BF16)
    ones_row = lax.broadcasted_iota(jnp.int32, (PAIR, PAIR), 0) // HD
    ones_col = lax.broadcasted_iota(jnp.int32, (PAIR, PAIR), 1) // HD
    blocks = (ones_row == ones_col).astype(F32).astype(BF16)
    high, mid, low = split_three(-(dot_nn(p_high, blocks) + dot_nn(p_low, blocks)))
    offsets = jnp.where(
        within == 0, high, jnp.where(within == 1, mid, jnp.where(within == 2, low, 0.0))
    ).astype(BF16)
    stats = st_ref[0]
    query = q_ref[0]
    query_h = [query * half for half in halves]
    grads_h = [grads * half for half in halves]
    query_x = [jnp.concatenate([query_h[h], stats * halves[h]], axis=1) for h in range(2)]
    grads_x = [jnp.concatenate([grads_h[h], offsets * halves[h]], axis=1) for h in range(2)]
    key_t = key.T
    key_sum = jnp.zeros((1, PAIR), F32)
    value_sum = jnp.zeros((1, PAIR), F32)

    def products(i):
        c, h = divmod(i, 2)
        at = slice(c * KCHUNK, (c + 1) * KCHUNK)
        return dot_nt(keys[at], query_x[h]), dot_nt(values[at], grads_x[h])

    steps = 2 * (rows // KCHUNK)
    following = products(0)
    for i in range(steps):
        c, h = divmod(i, 2)
        at = slice(c * KCHUNK, (c + 1) * KCHUNK)
        scores, weight_grad = following
        if i + 1 < steps:
            following = products(i + 1)
        if h == 0:
            value_grad = jnp.zeros((KCHUNK, PAIR), F32)
            key_grad = jnp.zeros((KCHUNK, PAIR), F32)
        weights = jnp.exp2(scores)
        score_grad = (weights * weight_grad).astype(BF16)
        value_grad += dot_nn(weights.astype(BF16), grads_h[h])
        key_grad += dot_nn(score_grad, query_h[h])
        head = slice(h * HD, (h + 1) * HD)
        part = dot_nn(key_t[head, at], score_grad)
        if c == 0:
            dqt[head, :] = part
        else:
            dqt[head, :] += part
        if h == 1:
            key_grad = turn(key_grad * (1.0 / LOG2E), cos_ref[at, :], -sin_ref[at, :])
            dv_ref[0, at, :] = value_grad.astype(BF16)
            dk_ref[0, at, :] = key_grad.astype(BF16)
            value_sum += jnp.sum(value_grad, axis=0, keepdims=True)
            key_sum += jnp.sum(key_grad, axis=0, keepdims=True)
    query_grad = turn(dqt[...].T * (HD ** (-0.5)), cos_ref[...], -sin_ref[...])
    dq_ref[0] = query_grad.astype(BF16)
    sums_ref[0, 0:1, :] = jnp.sum(query_grad, axis=0, keepdims=True)
    sums_ref[0, 1:2, :] = key_sum
    sums_ref[0, 2:3, :] = value_sum


def gelu_parts(pre):
    magnitude = jnp.abs(pre)
    bell = jnp.exp2(pre * pre * (-0.5 * LOG2E))
    divisor = 1.0 + (0.3275911 / math.sqrt(2.0)) * magnitude
    t = pl.reciprocal(divisor, approx=True)
    t = t * (2.0 - divisor * t)
    poly = t * (
        0.5 * 0.254829592
        + t
        * (
            0.5 * -0.284496736
            + t * (0.5 * 1.421413741 + t * (0.5 * -1.453152027 + t * (0.5 * 1.061405429)))
        )
    )
    tail = poly * bell
    share = jnp.where(pre > 0.0, 1.0 - tail, tail)
    return pre * share, share + pre * bell * (1.0 / math.sqrt(2.0 * math.pi))


SIDE_ORDER = ("side", "s0", "s1")
SEQ_ORDER = ("s0", "s1", "side")


def scatter_plan(order):
    plan = []
    names = ("core", "side", "s0", "s1")
    for number in range(1 << len(names)):
        bits = {name: number >> i & 1 for i, name in enumerate(names)}
        slot = 0
        for name in order:
            slot = slot * 2 + bits[name]
        plan.append((bits["core"] + 2 * bits["side"], bits["s0"] + 2 * bits["s1"], bits["core"], slot))
    return plan


def feed_kernel(count, orders, meta, *refs):
    toks, cots, refs = refs[:count], refs[count : 2 * count], refs[2 * count :]
    square_pieces, refs = refs[:PIECES], refs[PIECES:]
    block_pieces, refs = refs[:PIECES], refs[PIECES:]
    ctx, vec, b_up, refs = refs[0], refs[1], refs[2], refs[3:]
    mixed_refs, refs = refs[:count], refs[count:]
    mg_ref, dctx_ref, vec_ref, up_stay, up_leave, down_stay, down_leave = refs[:7]
    (
        tok_buf,
        cot_buf,
        mix_buf,
        w_out,
        w_up,
        w_down,
        hid,
        slope,
        dup,
        ddown,
        dout,
        standard,
        acc,
        normed,
        normed_t,
        grad_low,
        grad_t,
        ctx_t,
        inverse,
        tok_sems,
        cot_sems,
        mix_sems,
        w_sems,
        sems,
    ) = refs[7:]
    step = pl.program_id(0)
    _, slots, portion, width = tok_buf.shape
    groups = w_up.shape[0]
    total_rows = slots * portion
    chunks = [slice(f, f + FCHUNK) for f in range(0, width, FCHUNK)]
    first_row = (step ^ meta[0]) * portion
    early = head_copies(meta, square_pieces, 3, w_out, w_sems, 0)
    late = block_copies(meta, block_pieces, 0, w_up, w_sems, HEAD_COPIES)
    late += block_copies(meta, block_pieces, 1, w_down, w_sems, HEAD_COPIES + PIECES)

    @pl.when(step == 0)
    def _():
        for copy in early + late:
            copy.start()

    fetch(step, toks, tok_buf, tok_sems)
    fetch(step, cots, cot_buf, cot_sems)

    def mix_copy(k):
        return pltpu.make_async_copy(mix_buf.at[0], mixed_refs[k], mix_sems.at[k % 2])

    @pl.when(step == 0)
    def _():
        for ref in (dup, ddown, dout, vec_ref, hid, grad_t):
            ref[...] = jnp.zeros_like(ref)
        for copy in early + late:
            copy.wait()

    for k in range(1, count):
        @pl.when(step == k)
        def _(k=k):
            mix_copy(k - 1).wait()

    spots = [(j, at) for j in range(groups) for at in chunks]
    per = len(chunks)
    parity = step % 2
    strips = []
    for n in range(slots):
        for inner in range(0, portion, STRIP):
            index = lax.broadcasted_iota(jnp.int32, (STRIP, 1), 0) + first_row + inner
            first = n * portion + inner
            strips.append(
                (slice(first, first + STRIP), n, slice(inner, inner + STRIP), index < meta[2 + n])
            )
    assert len(strips) == groups and len(spots) == 3 * groups

    def normalize(at, slot, inner, alive):
        middle = tok_buf[parity, slot, inner, :].astype(F32) + acc[at, :] + vec[3:4, :]
        std, inv = standardize(middle)
        standard[at, :] = std
        inverse[at, :] = jnp.broadcast_to(inv, (STRIP, PAIR))
        acc[at, :] = middle + vec[4:5, :]
        normed[at, :] = (std * vec[7:8, :] + vec[8:9, :]).astype(BF16)

    def take_grad(at, slot, inner, alive):
        out_grad = jnp.where(alive, cot_buf[parity, slot, inner, :].astype(F32), 0.0)
        vec_ref[4:5, :] += jnp.sum(out_grad, axis=0, keepdims=True)
        grad_low[at, :] = out_grad.astype(BF16)
        normed_t[:, at] = normed[at, :].T

    def finish(at, slot, inner, alive):
        mix_buf[0, slot, inner, :] = jnp.where(alive, acc[at, :], 0.0).astype(BF16)

    def denormalize(at, slot, inner, alive):
        norm_grad, std = acc[at, :], standard[at, :]
        vec_ref[7:8, :] += jnp.sum(norm_grad * std, axis=0, keepdims=True)
        vec_ref[8:9, :] += jnp.sum(norm_grad, axis=0, keepdims=True)
        scaled = norm_grad * vec[7:8, :]
        middle_grad = grad_low[at, :].astype(F32) + inverse[at, 0:1] * (
            scaled
            - jnp.mean(scaled, axis=-1, keepdims=True)
            - std * jnp.mean(scaled * std, axis=-1, keepdims=True)
        )
        vec_ref[3:4, :] += jnp.sum(middle_grad, axis=0, keepdims=True)
        mg_ref[slot, inner, :] = middle_grad.astype(BF16)

    def up_dot(i):
        j, at = spots[i]
        return dot_nn(normed[...], w_up[j, :, at])

    def hidden_dot(i):
        j, at = spots[i]
        return dot_nt(grad_low[...], w_down[j, at, :])

    acc[...] = dot_nn(ctx[...].reshape(total_rows, width), w_out[...])
    for s, strip in enumerate(strips):
        normalize(*strip)
        ddown[s] += dot_nn(grad_t[...], hid[s])

    following = up_dot(0)
    for i, (j, at) in enumerate(spots):
        pre = following + b_up[j, :, at]
        if i + 1 < len(spots):
            following = up_dot(i + 1)
        if i % per == per - 1 and j > 0:
            acc[...] += dot_nn(hid[j - 1], w_down[j - 1])
        rows_at, slot, inner, _ = strips[i % groups]
        if i < groups:
            take_grad(*strips[i])
        elif i < 2 * groups:
            grad_t[:, rows_at] = grad_low[rows_at, :].T
        else:
            ctx_t[:, rows_at] = ctx[slot, inner, :].T
        hidden, bend = gelu_parts(pre)
        hid[j, :, at] = hidden.astype(BF16)
        slope[j, :, at] = bend.astype(BF16)

    following = hidden_dot(0)
    acc[...] += dot_nn(hid[groups - 1], w_down[groups - 1])
    for i, (j, at) in enumerate(spots):
        back = following
        if i + 1 < len(spots):
            following = hidden_dot(i + 1)
        if i < groups // 2:
            finish(*strips[2 * i])
            finish(*strips[2 * i + 1])
        if i % per == 0 and j > 0:
            part = dot_nt(slope[j - 1], w_up[j - 1])
            if j == 1:
                acc[...] = part
            else:
                acc[...] += part
        pre_grad = back * slope[j, :, at].astype(F32)
        vec_ref[9 + j : 10 + j, at] += jnp.sum(pre_grad, axis=0, keepdims=True)
        slope[j, :, at] = pre_grad.astype(BF16)
    acc[...] += dot_nt(slope[groups - 1], w_up[groups - 1])

    def turn_back(s, carry):
        per_slot = portion // STRIP
        at = pl.ds(aligned(s * STRIP, STRIP), STRIP)
        denormalize(at, s // per_slot, pl.ds(aligned(s % per_slot * STRIP, STRIP), STRIP), None)
        dup[s] += dot_nn(normed_t[...], slope[s])
        return carry

    lax.fori_loop(0, groups, turn_back, 0)
    middle_low = mg_ref[...].reshape(total_rows, width)
    dctx_ref[...] = dot_nt(middle_low, w_out[...]).astype(BF16).reshape(slots, portion, width)
    dout[...] += dot_nn(ctx_t[...], middle_low)
    for k in range(count):
        @pl.when(step == k)
        def _(k=k):
            mix_copy(k).start()

    @pl.when(step == pl.num_programs(0) - 1)
    def _():
        mix_copy(count - 1).wait()

        def last_share(j, carry):
            ddown[j] += dot_nn(grad_t[...], hid[j])
            return carry

        lax.fori_loop(0, groups, last_share, 0)

    @pl.when(step == pl.num_programs(0) - 1)
    def _():
        here, position = meta[0], meta[1] % PARTS
        size = width // PARTS
        per_block = hid.shape[1] // size
        ring = hid.shape[0] * per_block
        o_size = HEADS_EACH * UNIT
        o_per_block = slope.shape[1] // o_size
        copies, o_copies = [], []
        for source, order, stay, leave in (
            (dup, orders[0], up_stay, up_leave),
            (ddown, orders[1], down_stay, down_leave),
        ):
            for block, part, away, slot in scatter_plan(order):
                number = len(copies) % ring
                if len(copies) >= ring:
                    copies[-ring].wait()
                stage = hid.at[number // per_block, pl.ds(number % per_block * size, size)]
                first = aligned((part ^ position) * size, size)
                stage[...] = source[here ^ block, pl.ds(first, size), :].astype(BF16)
                target = leave if away else stay
                copies.append(
                    pltpu.make_async_copy(stage, target.at[slot, pl.ds(0, size)], sems.at[number])
                )
                copies[-1].start()
                if source is dup:
                    continue
                number = len(o_copies)
                stage = slope.at[
                    number // o_per_block, pl.ds(number % o_per_block * o_size, o_size)
                ]
                for i in range(HEADS_EACH):
                    first = (i * HEAD_DEVICES + (here ^ block)) * HD + (part ^ position) * UNIT
                    stage[i * UNIT : (i + 1) * UNIT, :] = dout[
                        pl.ds(aligned(first, UNIT), UNIT), :
                    ].astype(BF16)
                o_copies.append(
                    pltpu.make_async_copy(
                        stage, target.at[slot, pl.ds(size, o_size)], sems.at[ring + number]
                    )
                )
                o_copies[-1].start()
        for copy in copies[-ring:] + o_copies:
            copy.wait()


def weight_kernel(columns, heads, meta, *refs):
    grads, refs = refs[: 3 * columns], refs[3 * columns :]
    normed, outs, acc = refs[0], refs[1:-1], refs[-1]
    step = pl.program_id(0)
    total_rows = normed.shape[0] * normed.shape[1]
    width = normed.shape[2]

    @pl.when(step == 0)
    def _():
        acc[...] = jnp.zeros_like(acc)

    turned = [
        grads[3 * p + i][...].reshape(total_rows, grads[3 * p + i].shape[-1]).T
        for i in range(3)
        for p in range(columns)
    ]
    acc[...] += dot_nn(jnp.concatenate(turned, axis=0), normed[...].reshape(total_rows, width))

    @pl.when(step == pl.num_programs(0) - 1)
    def _():
        here, side = meta[0], meta[1] % 2
        unit = HD // 2
        for block, out in enumerate(outs):
            for part in range(2):
                for i in range(3):
                    for head in range(heads):
                        first = ((i * heads + head) * HEAD_DEVICES + (here ^ block)) * HD
                        first = aligned(first + (part ^ side) * unit, unit)
                        place = (i * heads + head) * unit
                        out[part, place : place + unit, :] = acc[pl.ds(first, unit), :].astype(
                            BF16
                        )


def vectors_kernel(count, meta, *refs):
    pieces, (vec, bias_up, buffer, sems) = refs[:count], refs[count:]
    copies = [
        pltpu.make_async_copy(
            ref.at[pl.ds(ref.shape[0] - SMALL_ROWS, SMALL_ROWS)], buffer.at[k], sems.at[k]
        )
        for k, ref in enumerate(pieces)
    ]
    for copy in copies:
        copy.start()
    for copy in copies:
        copy.wait()
    values = [buffer[k].astype(F32) for k in range(count)]
    part = HEADS_EACH * HD
    vec[...] = jnp.zeros_like(vec)
    for g in range(count):
        at = meta[0] ^ g
        mine = values[0]
        for k in range(1, count):
            mine = jnp.where(at == k, values[k], mine)
        for i in range(13):
            row = mine[i // 4 : i // 4 + 1, i % 4 * part : (i % 4 + 1) * part]
            if i < 3:
                for head in range(HEADS_EACH):
                    place = (head * count + g) * HD
                    vec[i : i + 1, place : place + HD] = row[:, head * HD : (head + 1) * HD]
            elif i < 9:
                vec[i : i + 1, g * part : (g + 1) * part] = row
            else:
                bias_up[g, :, (i - 9) * part : (i - 8) * part] = row


def input_kernel(count, columns, opening, meta, *refs):
    toks, weights = refs[:count], refs[count : count + PIECES]
    refs = refs[count + PIECES :]
    grads, refs = refs[: 4 * columns], refs[4 * columns :]
    vec, vec_in, mg = refs[:3]
    out_refs, refs = refs[3 : 3 + count], refs[3 + count :]
    vec_ref, buffer, out_buf, wq, wk, wv, tok_sems, out_sems, w_sems = refs
    step = pl.program_id(0)
    _, slots, portion, width = buffer.shape
    total_rows = slots * portion
    copies = []
    for i, ref in enumerate((wq, wk, wv)):
        copies += head_copies(meta, weights, i, ref, w_sems, i * HEAD_COPIES)

    @pl.when(step == 0)
    def _():
        for copy in copies:
            copy.start()

    fetch(step, toks, buffer, tok_sems)

    @pl.when(step == 0)
    def _():
        vec_ref[...] = vec_in[...]
        if opening:
            for i in range(3):
                vec_ref[i : i + 1, :] = jnp.concatenate(
                    [
                        jnp.sum(grads[4 * p + 3][:, i, :], axis=0, keepdims=True)
                        for p in range(columns)
                    ],
                    axis=1,
                )
        for copy in copies:
            copy.wait()

    tok = buffer[step % 2].reshape(total_rows, width).astype(F32)
    standard, inverse = standardize(tok)
    norm_grad = jnp.zeros((total_rows, width), F32)
    for i, weight in enumerate((wq, wk, wv)):
        low = jnp.concatenate(
            [
                grads[4 * p + i][...].reshape(total_rows, grads[4 * p + i].shape[-1])
                for p in range(columns)
            ],
            axis=1,
        )
        norm_grad += dot_nn(low, weight[...])
    vec_ref[5:6, :] += jnp.sum(norm_grad * standard, axis=0, keepdims=True)
    vec_ref[6:7, :] += jnp.sum(norm_grad, axis=0, keepdims=True)
    scaled = norm_grad * vec[5:6, :]
    result = mg[...].reshape(total_rows, width).astype(F32) + inverse * (
        scaled
        - jnp.mean(scaled, axis=-1, keepdims=True)
        - standard * jnp.mean(scaled * standard, axis=-1, keepdims=True)
    )
    emit(step, result.astype(BF16).reshape(slots, portion, width), out_refs, out_buf, out_sems)


def rest_units(first_bits, inputs, position):
    near, far = inputs
    one, two = first_bits
    for number in range(PARTS):
        yield (
            number ^ position,
            far if number >> two & 1 else near,
            number >> one & 1,
        )


def unpack_up_kernel(first_bits, meta, near, far, out):
    size = out.shape[0] // PARTS
    for part, ref, index in rest_units(first_bits, (near, far), meta[1] % PARTS):
        out[pl.ds(aligned(part * size, 8), size), :] = ref[index].astype(F32)


def unpack_down_kernel(first_bits, meta, near, far, down, out, scratch):
    size = down.shape[0] // PARTS
    for part, ref, index in rest_units(first_bits, (near, far), meta[1] % PARTS):
        scratch[pl.ds(aligned(part * size, 8), size), :] = ref[index, :size, :].astype(F32)
        for i in range(HEADS_EACH):
            first = aligned(i * HD + part * UNIT, 8)
            unit = size + i * UNIT
            out[pl.ds(first, UNIT), :] = ref[index, unit : unit + UNIT, :].astype(F32)
    down[...] = scratch[...].T


def unpack_heads_kernel(early_heads, meta, near, far, near_late, far_late, *outs):
    unit = HD // 2
    for inputs, heads in (
        ((near, far), range(early_heads)),
        ((near_late, far_late), range(early_heads, HEADS_EACH)),
    ):
        for number, ref in enumerate(inputs):
            part = number ^ (meta[1] % 2)
            for i, out in enumerate(outs):
                for place, head in enumerate(heads):
                    first = aligned(head * HD + part * unit, 8)
                    at = (i * len(heads) + place) * unit
                    out[pl.ds(first, unit), :] = ref[0, at : at + unit, :].astype(F32)


def place_kernel(count, meta, *refs):
    out = refs[count]
    for k in range(count):
        out[:, meta[0] ^ k] = refs[k][...]


def whole(shape):
    return pl.BlockSpec(
        shape, lambda *_: (0,) * len(shape), pipeline_mode=pl.Buffered(buffer_count=1)
    )


ANYWHERE = pl.BlockSpec(memory_space=pl.ANY)


def call(kernel, name, meta, args, grid, in_specs, out_specs, out_shape, scratch=(), cost=None, aliases=None):
    return pl.pallas_call(
        kernel,
        grid_spec=pltpu.PrefetchScalarGridSpec(
            num_scalar_prefetch=1,
            grid=grid,
            in_specs=in_specs,
            out_specs=out_specs,
            scratch_shapes=list(scratch),
        ),
        out_shape=out_shape,
        compiler_params=pltpu.CompilerParams(vmem_limit_bytes=LIMIT),
        cost_estimate=pl.CostEstimate(flops=1, bytes_accessed=1, transcendentals=0),
        input_output_aliases=aliases or {},
        name=name,
    )(meta, *args)


def local(
    tokens,
    cotangent,
    lengths,
    owners,
    codons,
    ln1_gain,
    ln1_bias,
    w_query,
    b_query,
    w_key,
    b_key,
    w_value,
    b_value,
    w_out,
    b_out,
    ln2_gain,
    ln2_bias,
    w_up,
    b_up,
    w_down,
    b_down,
):
    heads = lax.axis_size("head")
    peers = lax.axis_size("seq")
    here = lax.axis_index("head").astype(jnp.int32)
    position = lax.axis_index("seq").astype(jnp.int32)
    total_slots, portion, width = tokens.shape
    slots = total_slots // heads
    rows = portion * heads
    part_width = ln1_gain.shape[0]
    assert heads == HEAD_DEVICES and part_width == HEADS_EACH * HD
    assert peers >= PARTS and peers & peers - 1 == 0
    peer_bits = peers.bit_length() - 1

    def tie(*values):
        return lax.optimization_barrier(values)

    def swap(array, bits, axis="head"):
        size = lax.axis_size(axis)
        return lax.ppermute(array, axis, [(i, i ^ bits) for i in range(size)])

    def move(array, name):
        if name == "core":
            return swap(array, 1)
        if name == "side":
            return swap(array, 2)
        return swap(array, 1 << int(name[1:]), "seq")

    def add(one, other):
        return (one.astype(F32) + other.astype(F32)).astype(BF16)


    def row_slices(array):
        view = array.reshape(slots, heads, portion, width)
        return [
            lax.dynamic_index_in_dim(view, here ^ k, 1, keepdims=False).reshape(
                slots * portion, width
            )
            for k in range(heads)
        ]

    def send_rows(pieces):
        moved = {k: swap(pieces[k], k) for k in (2, 3, 1)}
        return [pieces[0]] + [moved[k] for k in range(1, heads)]

    def gather(shard):
        half = shard.shape[1] // 2
        mine = lax.dynamic_slice_in_dim(shard, position % 2 * half, half, 1)
        across = swap(mine, 2)
        beside = swap(across, 1, "seq")
        return [shard, swap(shard, 1), across, beside, swap(across, 1), swap(beside, 1)]

    named = 9
    packed = jnp.concatenate(
        [b_query, b_key, b_value, b_out, b_down, ln1_gain, ln1_bias, ln2_gain, ln2_bias, b_up]
        + [jnp.zeros((SMALL_ROWS * width - (named + heads) * part_width,), BF16)]
    ).reshape(SMALL_ROWS, width)
    token_slices = row_slices(tokens)
    square_parts = [w_query, w_key, w_value, w_out]
    square = jnp.concatenate(square_parts + [packed], axis=0)
    half_width = part_width // 2
    assert slots * portion == SQUARE_FIRST[2]
    first_load = jnp.concatenate(
        [token_slices[2]]
        + [
            lax.dynamic_slice_in_dim(part, position % 2 * half_width, half_width, 0)
            for part in square_parts
        ]
        + [packed],
        axis=0,
    )
    first_load, token_slices, square = tie(first_load, token_slices, square)
    first_across = swap(first_load, 2)
    tok_core = swap(token_slices[1], 1)
    square_core = swap(square, 1)
    first_across, tok_core, square_core = tie(first_across, tok_core, square_core)
    tok_far = swap(token_slices[3], 3)
    square_across = first_across[SQUARE_FIRST[2] :]
    square_beside = swap(square_across, 1, "seq")
    square_far = swap(square_across, 1)
    block = jnp.stack([w_up, w_down])
    block_half = lax.dynamic_slice_in_dim(block, position % 2 * (width // 2), width // 2, 1)
    square_beside, block, block_half, tok_far, square_far = tie(
        square_beside, block, block_half, tok_far, square_far
    )
    square_last = swap(square_beside, 1)
    block_across = swap(block_half, 2)
    block_core = swap(block, 1)
    cots = send_rows(row_slices(tie(cotangent, square_beside)[0]))
    squares = [square, square_core, first_across, square_beside, square_far, square_last]
    toks = [token_slices[0], tok_core, first_across, tok_far]

    own_lengths = lax.dynamic_index_in_dim(
        lengths.reshape(slots, heads), here, 1, keepdims=False
    ).astype(jnp.int32)
    meta = jnp.concatenate([here.reshape(1), position.reshape(1), own_lengths])

    vec, bias_up = call(
        functools.partial(vectors_kernel, heads),
        "vectors",
        meta,
        [squares[0], squares[1], squares[2], squares[4]],
        (1,),
        [ANYWHERE] * heads,
        [whole((VECTOR_ROWS, width)), whole((heads, 1, width))],
        [
            jax.ShapeDtypeStruct((VECTOR_ROWS, width), F32),
            jax.ShapeDtypeStruct((heads, 1, width), F32),
        ],
        [
            pltpu.VMEM((heads, SMALL_ROWS, width), BF16),
            pltpu.SemaphoreType.DMA((heads,)),
        ],
        cost=(0, 65536),
    )

    half = HD // 2
    frequency = 10000.0 ** (-(jnp.arange(half, dtype=F32) * 2.0 / HD))
    angles = jnp.arange(rows, dtype=F32)[:, None] * frequency[None, :]
    cos, sin = jnp.cos(angles), jnp.sin(angles)
    cos = jnp.concatenate([cos, cos, cos, cos], axis=1)
    sin = jnp.concatenate([-sin, sin, -sin, sin], axis=1)

    low = jax.ShapeDtypeStruct((slots, rows, width), BF16)
    piece = jax.ShapeDtypeStruct((slots, portion, width), BF16)
    vector = jax.ShapeDtypeStruct((VECTOR_ROWS, width), F32)
    work = slots * rows * width
    flat = pl.BlockSpec((slots, portion, width), lambda k, m: (0, k ^ m[0], 0))
    table = pl.BlockSpec((portion, PAIR), lambda k, m: (k ^ m[0], 0))
    square_buffer = pltpu.VMEM((width, width), BF16)
    pair_buffer = pltpu.VMEM((2, slots, portion, width), BF16)
    two = pltpu.SemaphoreType.DMA((2,))
    row_sems = pltpu.SemaphoreType.DMA((2, slots))
    three_heads = pltpu.SemaphoreType.DMA((3 * HEAD_COPIES,))
    vec_spec = whole((VECTOR_ROWS, width))
    vec_out = pl.BlockSpec((VECTOR_ROWS, width), lambda *_: (0, 0))

    normed, q, k, v = call(
        functools.partial(project_kernel, heads),
        "project",
        meta,
        [*toks, *squares, vec, cos, sin],
        (heads,),
        [ANYWHERE] * (heads + PIECES) + [vec_spec, table, table],
        [flat] * 4,
        [low] * 4,
        [pair_buffer, square_buffer, square_buffer, square_buffer, row_sems, three_heads],
        cost=(6 * work * width, 8 * work),
    )

    pairs = width // PAIR
    tile = pl.BlockSpec((1, rows, PAIR), lambda n, p, *_: (n, 0, p))

    def attend(meta, slot, before):
        picked = pl.BlockSpec((1, rows, PAIR), lambda p, *_: (slot, 0, p))
        return call(
            functools.partial(attend_kernel, slot),
            "attend",
            meta,
            [q, k, v, *before],
            (pairs,),
            [picked] * 3 + [ANYWHERE] * len(before),
            [picked] * 3,
            [low] * 3,
            cost=(16 * work * rows // slots, 10 * work // slots),
            aliases={4 + i: i for i in range(len(before))},
        )

    attended = []
    now = meta
    for slot in range(slots):
        if slot == 0:
            now, q, block_across = tie(now, q, block_across)
            block_beside = swap(block_across, 1, "seq")
            block_far = swap(block_across, 1)
        elif slot == 1:
            now, block_beside, attended, cots[2] = tie(meta, block_beside, attended, cots[2])
            blocks = [block, block_core, block_across, block_beside, block_far]
            blocks += [swap(block_beside, 1)]
        attended = attend(now, slot, attended)
    context, context_rest, stats = attended

    size = width // PARTS
    o_size = HEADS_EACH * UNIT
    up_shape = jax.ShapeDtypeStruct((2 * PARTS, size, width), BF16)
    down_shape = jax.ShapeDtypeStruct((2 * PARTS, size + o_size, width), BF16)
    ring = heads * (slots * portion // size)
    block_buffer = pltpu.VMEM((heads, width, width), BF16)
    block_sums = pltpu.VMEM((heads, width, width), F32)
    hidden_buffer = pltpu.VMEM((heads, slots * portion, width), BF16)
    row_sums = pltpu.VMEM((slots * portion, width), F32)
    row_buffer = pltpu.VMEM((slots * portion, width), BF16)
    turned_buffer = pltpu.VMEM((width, slots * portion), BF16)
    out = call(
        functools.partial(feed_kernel, heads, (SIDE_ORDER, SEQ_ORDER)),
        "feed",
        meta,
        [*toks, *cots, *squares, *blocks, context, vec, bias_up],
        (heads,),
        [ANYWHERE] * (2 * heads + 2 * PIECES) + [flat, vec_spec, whole((heads, 1, width))],
        [ANYWHERE] * heads + [flat, flat, vec_out] + [ANYWHERE] * 4,
        [piece] * heads + [low, low, vector] + [up_shape] * 2 + [down_shape] * 2,
        [
            pair_buffer,
            pair_buffer,
            pltpu.VMEM((1, slots, portion, width), BF16),
            square_buffer,
            block_buffer,
            block_buffer,
            hidden_buffer,
            hidden_buffer,
            block_sums,
            block_sums,
            pltpu.VMEM((width, width), F32),
            row_sums,
            row_sums,
            row_buffer,
            turned_buffer,
            row_buffer,
            turned_buffer,
            turned_buffer,
            pltpu.VMEM((slots * portion, PAIR), F32),
            row_sems,
            row_sems,
            two,
            pltpu.SemaphoreType.DMA((HEAD_COPIES + 2 * PIECES,)),
            pltpu.SemaphoreType.DMA((ring + 4 * PARTS,)),
        ],
        cost=(54 * work * width, 60 * MIB),
    )
    mixed, out = out[:heads], out[heads:]
    middle_grad, context_grad, feed_vec, up_stay, up_leave, down_stay, down_leave = out


    class Chain:
        def __init__(self, stay, leave, order, back):
            self.state = (stay, leave)
            self.stages = [("half", "core")] + [("half", name) for name in order]
            self.stages += [("full", f"s{bit}") for bit in range(PART_BITS, peer_bits)]
            self.stages += [("back", name) for name in back]
            self.done = 0
            self.first_bits = tuple(int(name[1:]) for name in back)

        @property
        def open(self):
            return self.done < len(self.stages)

        def start(self):
            self.got = move(self.state[1], self.stages[self.done][1])

        def absorb(self):
            kind = self.stages[self.done][0]
            self.done += 1
            if not self.open:
                self.ends = [self.state[0], self.got]
                return
            if kind == "back":
                current = jnp.concatenate([self.state[0], self.got], axis=0)
            else:
                current = add(self.state[0], self.got)
            if self.stages[self.done][0] == "half":
                count = current.shape[0] // 2
                self.state = (current[:count], current[count:])
            else:
                self.state = (current, current)

    class ShortChain:
        def __init__(self, outs, at_once):
            self.state = tuple(outs)
            self.stages = ["head"] if at_once else ["core", "side"]
            self.stages += ["half", "both"]
            self.stages += [f"s{bit}" for bit in range(3, peer_bits)] + ["back"]
            self.done = 0

        @property
        def open(self):
            return self.done < len(self.stages)

        def start(self):
            stage = self.stages[self.done]
            state = self.state
            if stage == "head":
                self.got = tuple(swap(state[k], k) for k in (2, 3, 1))
                self.kept = state[0]
            elif stage == "core":
                self.got = tuple(swap(state[k], 1) for k in (1, 3))
            elif stage == "side":
                self.got = (swap(state[1], 2),)
                self.kept = state[0]
            elif stage == "half":
                self.got = (move(state[1], "s0"),)
                self.kept = state[0]
            elif stage == "both":
                self.got = tuple(swap(state[0], k, "seq") for k in (4, 6, 2))
                self.kept = state[0]
            else:
                self.got = (move(state[0], "s0" if stage == "back" else stage),)
                self.kept = state[0]

        def absorb(self):
            stage = self.stages[self.done]
            self.done += 1
            if stage == "back":
                self.ends = [self.kept, self.got[0]]
                return
            if stage == "core":
                self.state = (add(self.state[0], self.got[0]), add(self.state[2], self.got[1]))
                return
            got = [array.astype(F32) for array in self.got]
            current = self.kept.astype(F32) + got[-1]
            if len(got) == 3:
                current = current + (got[0] + got[1])
            current = current.astype(BF16)
            if self.stages[self.done] == "half":
                self.state = (current[:1], current[1:])
            else:
                self.state = (current,)

    def mark(meta, chains, new=(), extras=()):
        meta, gots, extras = tie(meta, [chain.got for chain in chains], list(extras))
        for chain, got in zip(chains, gots):
            chain.got = got
            chain.absorb()
        active = [chain for chain in chains if chain.open] + list(new)
        meta, states = tie(meta, [chain.state for chain in [*chains, *new]])
        for chain, state in zip([*chains, *new], states):
            chain.state = state
        for chain in active:
            chain.start()
        return meta, active, extras

    up = Chain(up_stay, up_leave, SIDE_ORDER, ("s1", "s0"))
    down = Chain(down_stay, down_leave, SEQ_ORDER, ("s0", "s1"))
    wide_table = whole((rows, PAIR))
    grads = []

    def attend_back(meta, number):
        first, count = CALLS[number]
        shifted = pl.BlockSpec((1, rows, PAIR), lambda n, p, *_: (n, 0, p + first))
        own = pl.BlockSpec((1, rows, PAIR), lambda n, p, *_: (n, 0, p))
        short = jax.ShapeDtypeStruct((slots, rows, count * PAIR), BF16)
        grads.append(
            call(
                attend_back_kernel,
                "attend_back",
                meta,
                [q, k, v, context_grad, context, context_rest, stats, cos, sin],
                (slots, count),
                [shifted] * 7 + [wide_table] * 2,
                [own] * 3 + [pl.BlockSpec((1, 8, PAIR), lambda n, p, *_: (n, 0, p))],
                [short] * 3 + [jax.ShapeDtypeStruct((slots, 8, count * PAIR), F32)],
                [pltpu.VMEM((PAIR, rows), F32)],
                cost=(40 * work * rows * count // pairs, 18 * work * count // pairs),
            )
        )

    def column_spec(array):
        return pl.BlockSpec((slots, portion, array.shape[-1]), lambda k, m: (0, k ^ m[0], 0))

    def weight_chain(meta, parts, head_count, at_once):
        arrays = [array for part in parts for array in part[:3]]
        shape = (2, 3 * head_count * HD // 2, width)
        outs = call(
            functools.partial(weight_kernel, len(parts), head_count),
            "weight_back",
            meta,
            [*arrays, normed],
            (heads,),
            [column_spec(array) for array in arrays] + [flat],
            [pl.BlockSpec(shape, lambda *_: (0, 0, 0))] * heads,
            [jax.ShapeDtypeStruct(shape, BF16)] * heads,
            [pltpu.VMEM((3 * head_count * heads * HD, width), F32)],
            cost=(2 * work * head_count * heads * HD * 3, 8 * work),
        )
        return ShortChain(outs, at_once)

    def placed(meta, moved, name):
        shape = (slots, heads, portion, width)
        return call(
            functools.partial(place_kernel, heads),
            name,
            meta,
            moved,
            (1,),
            [whole((slots, portion, width))] * heads,
            whole(shape),
            jax.ShapeDtypeStruct(shape, BF16),
            cost=(0, 4 * work),
        ).reshape(total_slots, portion, width)

    now, active, _ = mark(meta, [], [up, down])
    attend_back(now, 0)
    now, active, _ = mark(tie(meta, grads[0])[0], active)
    attend_back(now, 1)
    now, active, _ = mark(tie(meta, grads[1])[0], active)
    now, mixed_two, mixed_three = tie(now, mixed[2], mixed[3])
    mixed_two, mixed_three = swap(mixed_two, 2), swap(mixed_three, 3)
    attend_back(now, 2)
    early = weight_chain(now, grads[:3], 2, False)
    now, active, _ = mark(tie(meta, grads[2], early.state)[0], active, [early])
    attend_back(now, 3)
    now, active, _ = mark(tie(meta, grads[3])[0], active)
    attend_back(now, 4)
    late = weight_chain(now, grads[3:], 1, True)
    now, active, (mixed_two, mixed_three) = mark(
        tie(meta, late.state)[0], active, [late], [mixed_two, mixed_three]
    )
    mixed_moved = [mixed[0], swap(mixed[1], 1), mixed_two, mixed_three]

    own_codons = lax.dynamic_index_in_dim(
        codons.reshape(slots, heads, rows), here, 1, keepdims=False
    )
    own_owners = lax.dynamic_index_in_dim(
        owners.reshape(slots, heads), here, 1, keepdims=False
    )
    live = jnp.arange(rows)[None, :] < own_lengths[:, None]
    matches = (own_codons[:, :, None] == jnp.arange(CODONS)[None, None, :]) & live[:, :, None]
    counts = jnp.sum(matches.astype(F32), axis=1)
    owned = (own_owners[None, :] == jnp.arange(peers)[:, None]).astype(F32)
    counts = jnp.sum(owned[:, :, None] * counts[None, :, :], axis=1).reshape(-1)
    free = (VECTOR_ROWS - named - heads) * width
    counts = jnp.pad(counts, (0, free - counts.shape[0])).reshape(-1, width)
    vec_in = jnp.concatenate([feed_vec[: named + heads], counts], axis=0)

    columns = len(CALLS)

    def input_back(meta, first, number, vec_in):
        chosen = pl.BlockSpec((slots, portion, width), lambda k, m: (0, (k + first) ^ m[0], 0))
        specs = []
        for part in grads:
            specs += [
                pl.BlockSpec(
                    (slots, portion, array.shape[-1]), lambda k, m: (0, (k + first) ^ m[0], 0)
                )
                for array in part[:3]
            ]
            specs += [whole(part[3].shape)]
        out = call(
            functools.partial(input_kernel, number, columns, first == 3),
            "input_back",
            meta,
            [
                *toks[first : first + number],
                *squares,
                *[array for part in grads for array in part],
                vec,
                vec_in,
                middle_grad,
            ],
            (number,),
            [ANYWHERE] * (number + PIECES) + specs + [vec_spec, vec_spec, chosen],
            [ANYWHERE] * number + [vec_out],
            [piece] * number + [vector],
            [
                pair_buffer,
                pair_buffer,
                square_buffer,
                square_buffer,
                square_buffer,
                row_sems,
                two,
                three_heads,
            ],
            cost=(6 * work * width * number // heads, 16 * work * number // heads),
        )
        return out[:number], out[number]

    (piece_three,), all_vec = input_back(now, 3, 1, vec_in)
    now, piece_three = tie(tie(meta, all_vec)[0], piece_three)
    piece_three = swap(piece_three, 3)
    now, active, _ = mark(now, active)
    (piece_two,), all_vec = input_back(now, 2, 1, all_vec)
    now, piece_two = tie(tie(meta, all_vec)[0], piece_two)
    piece_two = swap(piece_two, 2)
    now, active, (piece_three,) = mark(now, active, extras=[piece_three])
    (piece_own, piece_core), all_vec = input_back(now, 0, 2, all_vec)
    now, all_vec, piece_core = tie(now, all_vec, piece_core)
    piece_core = swap(piece_core, 1)
    now, active, (piece_two,) = mark(now, active, extras=[piece_two])
    while up.open or down.open:
        now, active, _ = mark(now, active)
    now, all_vec = tie(now, all_vec)
    one_vec = swap(all_vec, 1, "seq")
    mixed_out = placed(now, mixed_moved, "place_mixed")
    now, active, (one_vec, mixed_out) = mark(now, active, extras=[one_vec, mixed_out])
    all_vec = all_vec + one_vec
    seq_vec = [swap(all_vec, k, "seq") for k in (4, 6, 2)]
    input_out = placed(now, [piece_own, piece_core, piece_two, piece_three], "place_input")
    grad_up = call(
        functools.partial(unpack_up_kernel, up.first_bits),
        "unpack_up",
        now,
        up.ends,
        (1,),
        [whole(array.shape) for array in up.ends],
        whole((width, width)),
        jax.ShapeDtypeStruct((width, width), F32),
        cost=(0, 6 * width * width),
    )
    now, active, (*seq_vec, input_out, grad_up) = mark(
        now, active, extras=[*seq_vec, input_out, grad_up]
    )
    all_vec = (all_vec + seq_vec[2]) + (seq_vec[0] + seq_vec[1])
    for bit in range(3, peer_bits):
        all_vec = all_vec + swap(all_vec, 1 << bit, "seq")
    own_vec = [swap(all_vec, k) for k in (2, 3, 1)]
    grad_down, grad_out = call(
        functools.partial(unpack_down_kernel, down.first_bits),
        "unpack_down",
        now,
        down.ends,
        (1,),
        [whole(array.shape) for array in down.ends],
        [whole((width, width)), whole((part_width, width))],
        [
            jax.ShapeDtypeStruct((width, width), F32),
            jax.ShapeDtypeStruct((part_width, width), F32),
        ],
        [pltpu.VMEM((width, width), F32)],
        cost=(0, 8 * width * width),
    )
    while active:
        now, active, _ = mark(now, active)
    own_vec, grad_down = tie(own_vec, grad_down)
    all_vec = (all_vec + own_vec[2]) + (own_vec[0] + own_vec[1])

    def half_spec(array):
        return whole(array.shape)

    head_shape = jax.ShapeDtypeStruct((part_width, width), F32)
    sources = [*early.ends, *late.ends]
    grad_q, grad_k, grad_v = call(
        functools.partial(unpack_heads_kernel, 2),
        "unpack_heads",
        meta,
        sources,
        (1,),
        [half_spec(array) for array in sources],
        [whole((part_width, width))] * 3,
        [head_shape] * 3,
        cost=(0, 6 * width * width),
    )

    by_head = lax.dynamic_index_in_dim(
        all_vec[:3].reshape(3, HEADS_EACH, heads, HD), here, 2, keepdims=False
    ).reshape(3, part_width)
    sums = lax.dynamic_slice_in_dim(all_vec[3:named], here * part_width, part_width, 1)
    dbq, dbk, dbv = [by_head[i] for i in range(3)]
    dbo, dbd, dg1, db1, dg2, db2 = [sums[i] for i in range(named - 3)]
    grad_b_up = lax.dynamic_index_in_dim(all_vec[named:], here, 0, keepdims=False)
    histogram = lax.dynamic_slice_in_dim(
        all_vec[named + heads :].reshape(1, -1), position * CODONS, CODONS, 1
    ).astype(jnp.int32)
    return (
        mixed_out,
        input_out,
        dg1,
        db1,
        grad_q,
        dbq,
        grad_k,
        dbk,
        grad_v,
        dbv,
        grad_out,
        dbo,
        dg2,
        db2,
        grad_up,
        grad_b_up,
        grad_down,
        dbd,
        histogram,
    )


def solution(mesh):
    return jax.shard_map(
        local,
        mesh=mesh,
        in_specs=(
            P("seq", "head", None),
            P("seq", "head", None),
            P("seq"),
            P("seq"),
            P("seq", None),
            P("head"),
            P("head"),
            P("head", None),
            P("head"),
            P("head", None),
            P("head"),
            P("head", None),
            P("head"),
            P("head", None),
            P("head"),
            P("head"),
            P("head"),
            P(None, "head"),
            P("head"),
            P("head", None),
            P("head"),
        ),
        out_specs=(
            P("seq", "head", None),
            P("seq", "head", None),
            P("head"),
            P("head"),
            P("head", None),
            P("head"),
            P("head", None),
            P("head"),
            P("head", None),
            P("head"),
            P("head", None),
            P("head"),
            P("head"),
            P("head"),
            P(None, "head"),
            P("head"),
            P("head", None),
            P("head"),
            P("seq", None),
        ),
        check_vma=False,
    )
```

```python
import functools
import math

import jax
import jax.numpy as jnp
from jax import lax
from jax.experimental import pallas as pl
from jax.experimental.pallas import tpu as pltpu
from jax.sharding import PartitionSpec as P

HD = 64
CODONS = 64
EPSILON = 1e-05
NEGATIVE = -1e30
PAIR = 2 * HD
LOG2E = 1.4426950408889634
QUERY_SCALE = HD ** (-0.5) * LOG2E
QCHUNK = 256
KCHUNK = 512
FCHUNK = 256
STRIP = 128
CALLS = ((0, 1), (1, 2), (3, 1), (4, 1), (5, 1))
PART_BITS = 2
PARTS = 1 << PART_BITS
UNIT = 16
VECTOR_ROWS = 16
SMALL_ROWS = 16

F32 = jnp.float32
BF16 = jnp.bfloat16
MIB = 1024 * 1024
LIMIT = 60 * MIB


def dot_nn(a, b):
    return lax.dot_general(a, b, (((1,), (0,)), ((), ())), preferred_element_type=F32)


def dot_nt(a, b):
    return lax.dot_general(a, b, (((1,), (1,)), ((), ())), preferred_element_type=F32)


def standardize(rows):
    center = jnp.mean(rows, axis=-1, keepdims=True)
    shifted = rows - center
    inverse = lax.rsqrt(jnp.mean(shifted * shifted, axis=-1, keepdims=True) + EPSILON)
    return shifted * inverse, inverse


def turn(tile, cos, sin):
    lane = lax.broadcasted_iota(jnp.int32, tile.shape, 1)
    swapped = jnp.where(
        lane % HD < HD // 2,
        pltpu.roll(tile, PAIR - HD // 2, 1),
        pltpu.roll(tile, HD // 2, 1),
    )
    return tile * cos + swapped * sin


def split_three(value):
    high = value.astype(BF16).astype(F32)
    rest = value - high
    mid = rest.astype(BF16).astype(F32)
    return high, mid, rest - mid


def aligned(value, multiple):
    return pl.multiple_of(value, multiple)


class RowCopy:
    def __init__(self, piece, target, sems):
        slots, portion, _ = target.shape
        self.copies = [
            pltpu.make_async_copy(
                piece.at[pl.ds(n * portion, portion)], target.at[n], sems.at[n]
            )
            for n in range(slots)
        ]

    def start(self):
        for copy in self.copies:
            copy.start()

    def wait(self):
        for copy in self.copies:
            copy.wait()


def fetch(step, pieces, buffer, sems):
    copies = [
        RowCopy(pieces[k], buffer.at[k % 2], sems.at[k % 2]) for k in range(len(pieces))
    ]

    @pl.when(step == 0)
    def _():
        copies[0].start()

    for k, copy in enumerate(copies):
        @pl.when(step == k - 1)
        def _(copy=copy):
            copy.start()

    for k, copy in enumerate(copies):
        @pl.when(step == k)
        def _(copy=copy):
            copy.wait()


def emit(step, value, targets, buffer, sems):
    copies = [
        pltpu.make_async_copy(buffer.at[k % 2], targets[k], sems.at[k % 2])
        for k in range(len(targets))
    ]
    last = len(copies) - 1
    for k in range(2, len(copies)):
        @pl.when(step == k)
        def _(k=k):
            copies[k - 2].wait()

    buffer[step % 2] = value
    for k, copy in enumerate(copies):
        @pl.when(step == k)
        def _(copy=copy):
            copy.start()

    @pl.when(step == last)
    def _():
        for copy in copies[max(last - 1, 0) :]:
            copy.wait()


def weight_plan(meta, rows):
    here, side = meta[0], meta[1] % 2
    half = rows // 2
    return [
        (0, here, 0, rows),
        (1, here ^ 1, 0, rows),
        (2, here ^ 2, side * half, half),
        (3, here ^ 2, (1 - side) * half, half),
        (4, here ^ 3, side * half, half),
        (5, here ^ 3, (1 - side) * half, half),
    ]


def head_copies(meta, pieces, which, target, sems, base):
    copies = []
    for i, block, offset, size in weight_plan(meta, HEADS_EACH * HD):
        step = size // HEADS_EACH
        for c in range(HEADS_EACH):
            row = offset + c * step
            place = (row // HD * HEAD_DEVICES + block) * HD + row % HD
            copies.append(
                pltpu.make_async_copy(
                    pieces[i].at[pl.ds(SQUARE_FIRST[i] + which * size + c * step, step)],
                    target.at[pl.ds(aligned(place, UNIT), step)],
                    sems.at[base + len(copies)],
                )
            )
    return copies


def block_copies(meta, pieces, which, target, sems, base):
    return [
        pltpu.make_async_copy(
            pieces[i].at[which],
            target.at[block, pl.ds(aligned(offset, UNIT), size)],
            sems.at[base + i],
        )
        for i, block, offset, size in weight_plan(meta, pieces[0].shape[1])
    ]


HEADS_EACH = 3
HEAD_DEVICES = 4
SQUARE_FIRST = (0, 0, 512, 0, 0, 0)
PIECES = 6
HEAD_COPIES = PIECES * HEADS_EACH


def project_kernel(count, meta, *refs):
    toks, weights = refs[:count], refs[count : count + PIECES]
    vec, cos_ref, sin_ref = refs[count + PIECES : count + PIECES + 3]
    n_out, q_out, k_out, v_out, buffer, wq, wk, wv, tok_sems, sems = refs[count + PIECES + 3 :]
    step = pl.program_id(0)
    _, slots, portion, width = buffer.shape
    copies = []
    for i, ref in enumerate((wq, wk, wv)):
        copies += head_copies(meta, weights, i, ref, sems, i * HEAD_COPIES)

    @pl.when(step == 0)
    def _():
        for copy in copies:
            copy.start()

    fetch(step, toks, buffer, tok_sems)
    tok = buffer[step % 2].reshape(slots * portion, width).astype(F32)
    standard, _ = standardize(tok)
    normed = (standard * vec[5:6, :] + vec[6:7, :]).astype(BF16)
    n_out[...] = normed.reshape(slots, portion, width)

    @pl.when(step == 0)
    def _():
        for copy in copies:
            copy.wait()

    cos = jnp.concatenate([cos_ref[...]] * slots, axis=0)
    sin = jnp.concatenate([sin_ref[...]] * slots, axis=0)
    query = dot_nt(normed, wq[...]) + vec[0:1, :]
    key = dot_nt(normed, wk[...]) + vec[1:2, :]
    for j in range(width // PAIR):
        at = slice(j * PAIR, (j + 1) * PAIR)
        q_out[:, :, at] = (
            (turn(query[:, at], cos, sin) * QUERY_SCALE)
            .astype(BF16)
            .reshape(slots, portion, PAIR)
        )
        k_out[:, :, at] = (
            turn(key[:, at], cos, sin).astype(BF16).reshape(slots, portion, PAIR)
        )
    value = dot_nt(normed, wv[...]) + vec[2:3, :]
    v_out[...] = value.astype(BF16).reshape(slots, portion, width)


def attend_kernel(slot, meta, q_ref, k_ref, v_ref, *refs):
    o_ref, rest_ref, st_ref = refs[-3:]
    length = meta[2 + slot]
    rows = k_ref.shape[1]
    lane = lax.broadcasted_iota(jnp.int32, (rows, PAIR), 1)
    place_in = lax.broadcasted_iota(jnp.int32, (rows, PAIR), 0)
    halves = [(lane // HD == h).astype(F32).astype(BF16) for h in range(2)]
    guard = jnp.where(
        lane % HD == 3, jnp.where(place_in < length, 0.0, NEGATIVE), 1.0
    ).astype(BF16)
    keys = jnp.concatenate([k_ref[0], guard], axis=1)
    values = v_ref[0]
    values_h = [values * half + (1.0 - half) for half in halves]
    short = (QCHUNK, PAIR)
    lane_c = lax.broadcasted_iota(jnp.int32, short, 1)
    first = lane_c < HD
    within = lane_c % HD
    flag = (lane_c == 3).astype(F32).astype(BF16)

    def scores_of(i):
        c, h = divmod(i, 2)
        at = slice(c * QCHUNK, (c + 1) * QCHUNK)
        query = jnp.concatenate([q_ref[0, at, :] * halves[h][:QCHUNK], flag], axis=1)
        return dot_nt(query, keys)

    steps = 2 * (rows // QCHUNK)
    following = scores_of(0)
    outs, logs = [], []
    for i in range(steps):
        c, h = divmod(i, 2)
        scores = following
        if i + 1 < steps:
            following = scores_of(i + 1)
        top = jnp.max(scores, axis=1, keepdims=True)
        weights = jnp.exp2(scores - top).astype(BF16)
        sums = dot_nn(weights, values_h[h])
        total = pltpu.roll(sums, HD, 1)
        outs.append(sums / total)
        logs.append(-top - jnp.log(total) * LOG2E)
        if h == 1:
            at = slice(c * QCHUNK, (c + 1) * QCHUNK)
            context = jnp.where(first, outs[0], outs[1])
            o_ref[0, at, :] = context.astype(BF16)
            rest_ref[0, at, :] = (context - context.astype(BF16).astype(F32)).astype(BF16)
            high, mid, low = split_three(jnp.where(first, logs[0], logs[1]))
            st_ref[0, at, :] = jnp.where(
                within == 0,
                high,
                jnp.where(
                    within == 1,
                    mid,
                    jnp.where(within == 2, low, jnp.where(within == 3, 1.0, 0.0)),
                ),
            ).astype(BF16)
            outs, logs = [], []


def attend_back_kernel(
    meta,
    q_ref,
    k_ref,
    v_ref,
    do_ref,
    o_ref,
    rest_ref,
    st_ref,
    cos_ref,
    sin_ref,
    dq_ref,
    dk_ref,
    dv_ref,
    sums_ref,
    dqt,
):
    length = meta[2 + pl.program_id(0)]
    rows = k_ref.shape[1]
    lane = lax.broadcasted_iota(jnp.int32, (rows, PAIR), 1)
    within = lane % HD
    place_in = lax.broadcasted_iota(jnp.int32, (rows, PAIR), 0)
    halves = [(lane // HD == h).astype(F32).astype(BF16) for h in range(2)]
    guard = jnp.where(within == 3, jnp.where(place_in < length, 0.0, NEGATIVE), 1.0).astype(BF16)
    key = k_ref[0]
    keys = jnp.concatenate([key, guard], axis=1)
    values = jnp.concatenate([v_ref[0], jnp.ones((rows, PAIR), BF16)], axis=1)
    grads = do_ref[0]
    product = grads.astype(F32) * (o_ref[0].astype(F32) + rest_ref[0].astype(F32))
    p_high = product.astype(BF16)
    p_low = (product - p_high.astype(F32)).astype(BF16)
    ones_row = lax.broadcasted_iota(jnp.int32, (PAIR, PAIR), 0) // HD
    ones_col = lax.broadcasted_iota(jnp.int32, (PAIR, PAIR), 1) // HD
    blocks = (ones_row == ones_col).astype(F32).astype(BF16)
    high, mid, low = split_three(-(dot_nn(p_high, blocks) + dot_nn(p_low, blocks)))
    offsets = jnp.where(
        within == 0, high, jnp.where(within == 1, mid, jnp.where(within == 2, low, 0.0))
    ).astype(BF16)
    stats = st_ref[0]
    query = q_ref[0]
    query_h = [query * half for half in halves]
    grads_h = [grads * half for half in halves]
    query_x = [jnp.concatenate([query_h[h], stats * halves[h]], axis=1) for h in range(2)]
    grads_x = [jnp.concatenate([grads_h[h], offsets * halves[h]], axis=1) for h in range(2)]
    key_t = key.T
    key_sum = jnp.zeros((1, PAIR), F32)
    value_sum = jnp.zeros((1, PAIR), F32)

    def products(i):
        c, h = divmod(i, 2)
        at = slice(c * KCHUNK, (c + 1) * KCHUNK)
        return dot_nt(keys[at], query_x[h]), dot_nt(values[at], grads_x[h])

    steps = 2 * (rows // KCHUNK)
    following = products(0)
    for i in range(steps):
        c, h = divmod(i, 2)
        at = slice(c * KCHUNK, (c + 1) * KCHUNK)
        scores, weight_grad = following
        if i + 1 < steps:
            following = products(i + 1)
        if h == 0:
            value_grad = jnp.zeros((KCHUNK, PAIR), F32)
            key_grad = jnp.zeros((KCHUNK, PAIR), F32)
        weights = jnp.exp2(scores)
        score_grad = (weights * weight_grad).astype(BF16)
        value_grad += dot_nn(weights.astype(BF16), grads_h[h])
        key_grad += dot_nn(score_grad, query_h[h])
        head = slice(h * HD, (h + 1) * HD)
        part = dot_nn(key_t[head, at], score_grad)
        if c == 0:
            dqt[head, :] = part
        else:
            dqt[head, :] += part
        if h == 1:
            key_grad = turn(key_grad * (1.0 / LOG2E), cos_ref[at, :], -sin_ref[at, :])
            dv_ref[0, at, :] = value_grad.astype(BF16)
            dk_ref[0, at, :] = key_grad.astype(BF16)
            value_sum += jnp.sum(value_grad, axis=0, keepdims=True)
            key_sum += jnp.sum(key_grad, axis=0, keepdims=True)
    query_grad = turn(dqt[...].T * (HD ** (-0.5)), cos_ref[...], -sin_ref[...])
    dq_ref[0] = query_grad.astype(BF16)
    sums_ref[0, 0:1, :] = jnp.sum(query_grad, axis=0, keepdims=True)
    sums_ref[0, 1:2, :] = key_sum
    sums_ref[0, 2:3, :] = value_sum


def gelu_parts(pre):
    magnitude = jnp.abs(pre)
    bell = jnp.exp2(pre * pre * (-0.5 * LOG2E))
    divisor = 1.0 + (0.3275911 / math.sqrt(2.0)) * magnitude
    t = pl.reciprocal(divisor, approx=True)
    t = t * (2.0 - divisor * t)
    poly = t * (
        0.5 * 0.254829592
        + t
        * (
            0.5 * -0.284496736
            + t * (0.5 * 1.421413741 + t * (0.5 * -1.453152027 + t * (0.5 * 1.061405429)))
        )
    )
    tail = poly * bell
    share = jnp.where(pre > 0.0, 1.0 - tail, tail)
    return pre * share, share + pre * bell * (1.0 / math.sqrt(2.0 * math.pi))


SIDE_ORDER = ("side", "s0", "s1")
SEQ_ORDER = ("s0", "s1", "side")


def scatter_plan(order):
    plan = []
    names = ("core", "side", "s0", "s1")
    for number in range(1 << len(names)):
        bits = {name: number >> i & 1 for i, name in enumerate(names)}
        slot = 0
        for name in order:
            slot = slot * 2 + bits[name]
        plan.append((bits["core"] + 2 * bits["side"], bits["s0"] + 2 * bits["s1"], bits["core"], slot))
    return plan


def feed_kernel(count, orders, meta, *refs):
    toks, cots, refs = refs[:count], refs[count : 2 * count], refs[2 * count :]
    square_pieces, refs = refs[:PIECES], refs[PIECES:]
    block_pieces, refs = refs[:PIECES], refs[PIECES:]
    ctx, vec, b_up, refs = refs[0], refs[1], refs[2], refs[3:]
    mixed_refs, refs = refs[:count], refs[count:]
    mg_ref, dctx_ref, vec_ref, up_stay, up_leave, down_stay, down_leave = refs[:7]
    (
        tok_buf,
        cot_buf,
        mix_buf,
        w_out,
        w_up,
        w_down,
        hid,
        slope,
        dup,
        ddown,
        dout,
        standard,
        acc,
        normed,
        normed_t,
        grad_low,
        grad_t,
        ctx_t,
        inverse,
        tok_sems,
        cot_sems,
        mix_sems,
        w_sems,
        sems,
    ) = refs[7:]
    step = pl.program_id(0)
    _, slots, portion, width = tok_buf.shape
    groups = w_up.shape[0]
    total_rows = slots * portion
    chunks = [slice(f, f + FCHUNK) for f in range(0, width, FCHUNK)]
    first_row = (step ^ meta[0]) * portion
    early = head_copies(meta, square_pieces, 3, w_out, w_sems, 0)
    late = block_copies(meta, block_pieces, 0, w_up, w_sems, HEAD_COPIES)
    late += block_copies(meta, block_pieces, 1, w_down, w_sems, HEAD_COPIES + PIECES)

    @pl.when(step == 0)
    def _():
        for copy in early + late:
            copy.start()

    fetch(step, toks, tok_buf, tok_sems)
    fetch(step, cots, cot_buf, cot_sems)

    def mix_copy(k):
        return pltpu.make_async_copy(mix_buf.at[0], mixed_refs[k], mix_sems.at[k % 2])

    @pl.when(step == 0)
    def _():
        for ref in (dup, ddown, dout, vec_ref, hid, grad_t):
            ref[...] = jnp.zeros_like(ref)
        for copy in early + late:
            copy.wait()

    for k in range(1, count):
        @pl.when(step == k)
        def _(k=k):
            mix_copy(k - 1).wait()

    spots = [(j, at) for j in range(groups) for at in chunks]
    per = len(chunks)
    parity = step % 2
    strips = []
    for n in range(slots):
        for inner in range(0, portion, STRIP):
            index = lax.broadcasted_iota(jnp.int32, (STRIP, 1), 0) + first_row + inner
            first = n * portion + inner
            strips.append(
                (slice(first, first + STRIP), n, slice(inner, inner + STRIP), index < meta[2 + n])
            )
    assert len(strips) == groups and len(spots) == 3 * groups

    def normalize(at, slot, inner, alive):
        middle = tok_buf[parity, slot, inner, :].astype(F32) + acc[at, :] + vec[3:4, :]
        std, inv = standardize(middle)
        standard[at, :] = std
        inverse[at, :] = jnp.broadcast_to(inv, (STRIP, PAIR))
        acc[at, :] = middle + vec[4:5, :]
        normed[at, :] = (std * vec[7:8, :] + vec[8:9, :]).astype(BF16)

    def take_grad(at, slot, inner, alive):
        out_grad = jnp.where(alive, cot_buf[parity, slot, inner, :].astype(F32), 0.0)
        vec_ref[4:5, :] += jnp.sum(out_grad, axis=0, keepdims=True)
        grad_low[at, :] = out_grad.astype(BF16)
        normed_t[:, at] = normed[at, :].T

    def finish(at, slot, inner, alive):
        mix_buf[0, slot, inner, :] = jnp.where(alive, acc[at, :], 0.0).astype(BF16)

    def denormalize(at, slot, inner, alive):
        norm_grad, std = acc[at, :], standard[at, :]
        vec_ref[7:8, :] += jnp.sum(norm_grad * std, axis=0, keepdims=True)
        vec_ref[8:9, :] += jnp.sum(norm_grad, axis=0, keepdims=True)
        scaled = norm_grad * vec[7:8, :]
        middle_grad = grad_low[at, :].astype(F32) + inverse[at, 0:1] * (
            scaled
            - jnp.mean(scaled, axis=-1, keepdims=True)
            - std * jnp.mean(scaled * std, axis=-1, keepdims=True)
        )
        vec_ref[3:4, :] += jnp.sum(middle_grad, axis=0, keepdims=True)
        mg_ref[slot, inner, :] = middle_grad.astype(BF16)

    def up_dot(i):
        j, at = spots[i]
        return dot_nn(normed[...], w_up[j, :, at])

    def hidden_dot(i):
        j, at = spots[i]
        return dot_nt(grad_low[...], w_down[j, at, :])

    acc[...] = dot_nn(ctx[...].reshape(total_rows, width), w_out[...])
    for s, strip in enumerate(strips):
        normalize(*strip)
        ddown[s] += dot_nn(grad_t[...], hid[s])

    following = up_dot(0)
    for i, (j, at) in enumerate(spots):
        pre = following + b_up[j, :, at]
        if i + 1 < len(spots):
            following = up_dot(i + 1)
        if i % per == per - 1 and j > 0:
            acc[...] += dot_nn(hid[j - 1], w_down[j - 1])
        rows_at, slot, inner, _ = strips[i % groups]
        if i < groups:
            take_grad(*strips[i])
        elif i < 2 * groups:
            grad_t[:, rows_at] = grad_low[rows_at, :].T
        else:
            ctx_t[:, rows_at] = ctx[slot, inner, :].T
        hidden, bend = gelu_parts(pre)
        hid[j, :, at] = hidden.astype(BF16)
        slope[j, :, at] = bend.astype(BF16)

    following = hidden_dot(0)
    acc[...] += dot_nn(hid[groups - 1], w_down[groups - 1])
    for i, (j, at) in enumerate(spots):
        back = following
        if i + 1 < len(spots):
            following = hidden_dot(i + 1)
        if i < groups // 2:
            finish(*strips[2 * i])
            finish(*strips[2 * i + 1])
        if i % per == 0 and j > 0:
            part = dot_nt(slope[j - 1], w_up[j - 1])
            if j == 1:
                acc[...] = part
            else:
                acc[...] += part
        pre_grad = back * slope[j, :, at].astype(F32)
        vec_ref[9 + j : 10 + j, at] += jnp.sum(pre_grad, axis=0, keepdims=True)
        slope[j, :, at] = pre_grad.astype(BF16)
    acc[...] += dot_nt(slope[groups - 1], w_up[groups - 1])

    def turn_back(s, carry):
        per_slot = portion // STRIP
        at = pl.ds(aligned(s * STRIP, STRIP), STRIP)
        denormalize(at, s // per_slot, pl.ds(aligned(s % per_slot * STRIP, STRIP), STRIP), None)
        dup[s] += dot_nn(normed_t[...], slope[s])
        return carry

    lax.fori_loop(0, groups, turn_back, 0)
    middle_low = mg_ref[...].reshape(total_rows, width)
    dctx_ref[...] = dot_nt(middle_low, w_out[...]).astype(BF16).reshape(slots, portion, width)
    dout[...] += dot_nn(ctx_t[...], middle_low)
    for k in range(count):
        @pl.when(step == k)
        def _(k=k):
            mix_copy(k).start()

    @pl.when(step == pl.num_programs(0) - 1)
    def _():
        mix_copy(count - 1).wait()

        def last_share(j, carry):
            ddown[j] += dot_nn(grad_t[...], hid[j])
            return carry

        lax.fori_loop(0, groups, last_share, 0)

    @pl.when(step == pl.num_programs(0) - 1)
    def _():
        here, position = meta[0], meta[1] % PARTS
        size = width // PARTS
        per_block = hid.shape[1] // size
        ring = hid.shape[0] * per_block
        o_size = HEADS_EACH * UNIT
        o_per_block = slope.shape[1] // o_size
        copies, o_copies = [], []
        for source, order, stay, leave in (
            (dup, orders[0], up_stay, up_leave),
            (ddown, orders[1], down_stay, down_leave),
        ):
            for block, part, away, slot in scatter_plan(order):
                number = len(copies) % ring
                if len(copies) >= ring:
                    copies[-ring].wait()
                stage = hid.at[number // per_block, pl.ds(number % per_block * size, size)]
                first = aligned((part ^ position) * size, size)
                stage[...] = source[here ^ block, pl.ds(first, size), :].astype(BF16)
                target = leave if away else stay
                copies.append(
                    pltpu.make_async_copy(stage, target.at[slot, pl.ds(0, size)], sems.at[number])
                )
                copies[-1].start()
                if source is dup:
                    continue
                number = len(o_copies)
                stage = slope.at[
                    number // o_per_block, pl.ds(number % o_per_block * o_size, o_size)
                ]
                for i in range(HEADS_EACH):
                    first = (i * HEAD_DEVICES + (here ^ block)) * HD + (part ^ position) * UNIT
                    stage[i * UNIT : (i + 1) * UNIT, :] = dout[
                        pl.ds(aligned(first, UNIT), UNIT), :
                    ].astype(BF16)
                o_copies.append(
                    pltpu.make_async_copy(
                        stage, target.at[slot, pl.ds(size, o_size)], sems.at[ring + number]
                    )
                )
                o_copies[-1].start()
        for copy in copies[-ring:] + o_copies:
            copy.wait()


def weight_kernel(columns, heads, meta, *refs):
    grads, refs = refs[: 3 * columns], refs[3 * columns :]
    normed, outs, acc = refs[0], refs[1:-1], refs[-1]
    step = pl.program_id(0)
    total_rows = normed.shape[0] * normed.shape[1]
    width = normed.shape[2]

    @pl.when(step == 0)
    def _():
        acc[...] = jnp.zeros_like(acc)

    turned = [
        grads[3 * p + i][...].reshape(total_rows, grads[3 * p + i].shape[-1]).T
        for i in range(3)
        for p in range(columns)
    ]
    acc[...] += dot_nn(jnp.concatenate(turned, axis=0), normed[...].reshape(total_rows, width))

    @pl.when(step == pl.num_programs(0) - 1)
    def _():
        here, side = meta[0], meta[1] % 2
        unit = HD // 2
        for block, out in enumerate(outs):
            for part in range(2):
                for i in range(3):
                    for head in range(heads):
                        first = ((i * heads + head) * HEAD_DEVICES + (here ^ block)) * HD
                        first = aligned(first + (part ^ side) * unit, unit)
                        place = (i * heads + head) * unit
                        out[part, place : place + unit, :] = acc[pl.ds(first, unit), :].astype(
                            BF16
                        )


def vectors_kernel(count, meta, *refs):
    pieces, (vec, bias_up, buffer, sems) = refs[:count], refs[count:]
    copies = [
        pltpu.make_async_copy(
            ref.at[pl.ds(ref.shape[0] - SMALL_ROWS, SMALL_ROWS)], buffer.at[k], sems.at[k]
        )
        for k, ref in enumerate(pieces)
    ]
    for copy in copies:
        copy.start()
    for copy in copies:
        copy.wait()
    values = [buffer[k].astype(F32) for k in range(count)]
    part = HEADS_EACH * HD
    vec[...] = jnp.zeros_like(vec)
    for g in range(count):
        at = meta[0] ^ g
        mine = values[0]
        for k in range(1, count):
            mine = jnp.where(at == k, values[k], mine)
        for i in range(13):
            row = mine[i // 4 : i // 4 + 1, i % 4 * part : (i % 4 + 1) * part]
            if i < 3:
                for head in range(HEADS_EACH):
                    place = (head * count + g) * HD
                    vec[i : i + 1, place : place + HD] = row[:, head * HD : (head + 1) * HD]
            elif i < 9:
                vec[i : i + 1, g * part : (g + 1) * part] = row
            else:
                bias_up[g, :, (i - 9) * part : (i - 8) * part] = row


def input_kernel(count, columns, opening, meta, *refs):
    toks, weights = refs[:count], refs[count : count + PIECES]
    refs = refs[count + PIECES :]
    grads, refs = refs[: 4 * columns], refs[4 * columns :]
    vec, vec_in, mg = refs[:3]
    out_refs, refs = refs[3 : 3 + count], refs[3 + count :]
    vec_ref, buffer, out_buf, wq, wk, wv, tok_sems, out_sems, w_sems = refs
    step = pl.program_id(0)
    _, slots, portion, width = buffer.shape
    total_rows = slots * portion
    copies = []
    for i, ref in enumerate((wq, wk, wv)):
        copies += head_copies(meta, weights, i, ref, w_sems, i * HEAD_COPIES)

    @pl.when(step == 0)
    def _():
        for copy in copies:
            copy.start()

    fetch(step, toks, buffer, tok_sems)

    @pl.when(step == 0)
    def _():
        vec_ref[...] = vec_in[...]
        if opening:
            for i in range(3):
                vec_ref[i : i + 1, :] = jnp.concatenate(
                    [
                        jnp.sum(grads[4 * p + 3][:, i, :], axis=0, keepdims=True)
                        for p in range(columns)
                    ],
                    axis=1,
                )
        for copy in copies:
            copy.wait()

    tok = buffer[step % 2].reshape(total_rows, width).astype(F32)
    standard, inverse = standardize(tok)
    norm_grad = jnp.zeros((total_rows, width), F32)
    for i, weight in enumerate((wq, wk, wv)):
        low = jnp.concatenate(
            [
                grads[4 * p + i][...].reshape(total_rows, grads[4 * p + i].shape[-1])
                for p in range(columns)
            ],
            axis=1,
        )
        norm_grad += dot_nn(low, weight[...])
    vec_ref[5:6, :] += jnp.sum(norm_grad * standard, axis=0, keepdims=True)
    vec_ref[6:7, :] += jnp.sum(norm_grad, axis=0, keepdims=True)
    scaled = norm_grad * vec[5:6, :]
    result = mg[...].reshape(total_rows, width).astype(F32) + inverse * (
        scaled
        - jnp.mean(scaled, axis=-1, keepdims=True)
        - standard * jnp.mean(scaled * standard, axis=-1, keepdims=True)
    )
    emit(step, result.astype(BF16).reshape(slots, portion, width), out_refs, out_buf, out_sems)


def rest_units(first_bits, inputs, position):
    near, far = inputs
    one, two = first_bits
    for number in range(PARTS):
        yield (
            number ^ position,
            far if number >> two & 1 else near,
            number >> one & 1,
        )


def unpack_up_kernel(first_bits, meta, near, far, out):
    size = out.shape[0] // PARTS
    for part, ref, index in rest_units(first_bits, (near, far), meta[1] % PARTS):
        out[pl.ds(aligned(part * size, 8), size), :] = ref[index].astype(F32)


def unpack_down_kernel(first_bits, meta, near, far, down, out, scratch):
    size = down.shape[0] // PARTS
    for part, ref, index in rest_units(first_bits, (near, far), meta[1] % PARTS):
        scratch[pl.ds(aligned(part * size, 8), size), :] = ref[index, :size, :].astype(F32)
        for i in range(HEADS_EACH):
            first = aligned(i * HD + part * UNIT, 8)
            unit = size + i * UNIT
            out[pl.ds(first, UNIT), :] = ref[index, unit : unit + UNIT, :].astype(F32)
    down[...] = scratch[...].T


def unpack_heads_kernel(early_heads, meta, near, far, near_late, far_late, *outs):
    unit = HD // 2
    for inputs, heads in (
        ((near, far), range(early_heads)),
        ((near_late, far_late), range(early_heads, HEADS_EACH)),
    ):
        for number, ref in enumerate(inputs):
            part = number ^ (meta[1] % 2)
            for i, out in enumerate(outs):
                for place, head in enumerate(heads):
                    first = aligned(head * HD + part * unit, 8)
                    at = (i * len(heads) + place) * unit
                    out[pl.ds(first, unit), :] = ref[0, at : at + unit, :].astype(F32)


def place_kernel(count, meta, *refs):
    out = refs[count]
    for k in range(count):
        out[:, meta[0] ^ k] = refs[k][...]


def whole(shape):
    return pl.BlockSpec(
        shape, lambda *_: (0,) * len(shape), pipeline_mode=pl.Buffered(buffer_count=1)
    )


ANYWHERE = pl.BlockSpec(memory_space=pl.ANY)


def call(kernel, name, meta, args, grid, in_specs, out_specs, out_shape, scratch=(), cost=None, aliases=None):
    return pl.pallas_call(
        kernel,
        grid_spec=pltpu.PrefetchScalarGridSpec(
            num_scalar_prefetch=1,
            grid=grid,
            in_specs=in_specs,
            out_specs=out_specs,
            scratch_shapes=list(scratch),
        ),
        out_shape=out_shape,
        compiler_params=pltpu.CompilerParams(vmem_limit_bytes=LIMIT),
        cost_estimate=pl.CostEstimate(flops=1, bytes_accessed=1, transcendentals=0),
        input_output_aliases=aliases or {},
        name=name,
    )(meta, *args)


def local(
    tokens,
    cotangent,
    lengths,
    owners,
    codons,
    ln1_gain,
    ln1_bias,
    w_query,
    b_query,
    w_key,
    b_key,
    w_value,
    b_value,
    w_out,
    b_out,
    ln2_gain,
    ln2_bias,
    w_up,
    b_up,
    w_down,
    b_down,
):
    heads = lax.axis_size("head")
    peers = lax.axis_size("seq")
    here = lax.axis_index("head").astype(jnp.int32)
    position = lax.axis_index("seq").astype(jnp.int32)
    total_slots, portion, width = tokens.shape
    slots = total_slots // heads
    rows = portion * heads
    part_width = ln1_gain.shape[0]
    assert heads == HEAD_DEVICES and part_width == HEADS_EACH * HD
    assert peers >= PARTS and peers & peers - 1 == 0
    peer_bits = peers.bit_length() - 1

    def tie(*values):
        return lax.optimization_barrier(values)

    def swap(array, bits, axis="head"):
        size = lax.axis_size(axis)
        return lax.ppermute(array, axis, [(i, i ^ bits) for i in range(size)])

    def move(array, name):
        if name == "core":
            return swap(array, 1)
        if name == "side":
            return swap(array, 2)
        return swap(array, 1 << int(name[1:]), "seq")

    def add(one, other):
        return (one.astype(F32) + other.astype(F32)).astype(BF16)


    def row_slices(array):
        view = array.reshape(slots, heads, portion, width)
        return [
            lax.dynamic_index_in_dim(view, here ^ k, 1, keepdims=False).reshape(
                slots * portion, width
            )
            for k in range(heads)
        ]

    def send_rows(pieces):
        moved = {k: swap(pieces[k], k) for k in (2, 3, 1)}
        return [pieces[0]] + [moved[k] for k in range(1, heads)]

    def gather(shard):
        half = shard.shape[1] // 2
        mine = lax.dynamic_slice_in_dim(shard, position % 2 * half, half, 1)
        across = swap(mine, 2)
        beside = swap(across, 1, "seq")
        return [shard, swap(shard, 1), across, beside, swap(across, 1), swap(beside, 1)]

    named = 9
    packed = jnp.concatenate(
        [b_query, b_key, b_value, b_out, b_down, ln1_gain, ln1_bias, ln2_gain, ln2_bias, b_up]
        + [jnp.zeros((SMALL_ROWS * width - (named + heads) * part_width,), BF16)]
    ).reshape(SMALL_ROWS, width)
    token_slices = row_slices(tokens)
    square_parts = [w_query, w_key, w_value, w_out]
    square = jnp.concatenate(square_parts + [packed], axis=0)
    half_width = part_width // 2
    assert slots * portion == SQUARE_FIRST[2]
    first_load = jnp.concatenate(
        [token_slices[2]]
        + [
            lax.dynamic_slice_in_dim(part, position % 2 * half_width, half_width, 0)
            for part in square_parts
        ]
        + [packed],
        axis=0,
    )
    first_load, token_slices, square = tie(first_load, token_slices, square)
    first_across = swap(first_load, 2)
    tok_core = swap(token_slices[1], 1)
    square_core = swap(square, 1)
    first_across, tok_core, square_core = tie(first_across, tok_core, square_core)
    tok_far = swap(token_slices[3], 3)
    square_across = first_across[SQUARE_FIRST[2] :]
    square_beside = swap(square_across, 1, "seq")
    square_far = swap(square_across, 1)
    block = jnp.stack([w_up, w_down])
    block_half = lax.dynamic_slice_in_dim(block, position % 2 * (width // 2), width // 2, 1)
    square_beside, block, block_half, tok_far, square_far = tie(
        square_beside, block, block_half, tok_far, square_far
    )
    square_last = swap(square_beside, 1)
    block_across = swap(block_half, 2)
    block_core = swap(block, 1)
    cots = send_rows(row_slices(tie(cotangent, square_beside)[0]))
    squares = [square, square_core, first_across, square_beside, square_far, square_last]
    toks = [token_slices[0], tok_core, first_across, tok_far]

    own_lengths = lax.dynamic_index_in_dim(
        lengths.reshape(slots, heads), here, 1, keepdims=False
    ).astype(jnp.int32)
    meta = jnp.concatenate([here.reshape(1), position.reshape(1), own_lengths])

    vec, bias_up = call(
        functools.partial(vectors_kernel, heads),
        "vectors",
        meta,
        [squares[0], squares[1], squares[2], squares[4]],
        (1,),
        [ANYWHERE] * heads,
        [whole((VECTOR_ROWS, width)), whole((heads, 1, width))],
        [
            jax.ShapeDtypeStruct((VECTOR_ROWS, width), F32),
            jax.ShapeDtypeStruct((heads, 1, width), F32),
        ],
        [
            pltpu.VMEM((heads, SMALL_ROWS, width), BF16),
            pltpu.SemaphoreType.DMA((heads,)),
        ],
        cost=(0, 65536),
    )

    half = HD // 2
    frequency = 10000.0 ** (-(jnp.arange(half, dtype=F32) * 2.0 / HD))
    angles = jnp.arange(rows, dtype=F32)[:, None] * frequency[None, :]
    cos, sin = jnp.cos(angles), jnp.sin(angles)
    cos = jnp.concatenate([cos, cos, cos, cos], axis=1)
    sin = jnp.concatenate([-sin, sin, -sin, sin], axis=1)

    low = jax.ShapeDtypeStruct((slots, rows, width), BF16)
    piece = jax.ShapeDtypeStruct((slots, portion, width), BF16)
    vector = jax.ShapeDtypeStruct((VECTOR_ROWS, width), F32)
    work = slots * rows * width
    flat = pl.BlockSpec((slots, portion, width), lambda k, m: (0, k ^ m[0], 0))
    table = pl.BlockSpec((portion, PAIR), lambda k, m: (k ^ m[0], 0))
    square_buffer = pltpu.VMEM((width, width), BF16)
    pair_buffer = pltpu.VMEM((2, slots, portion, width), BF16)
    two = pltpu.SemaphoreType.DMA((2,))
    row_sems = pltpu.SemaphoreType.DMA((2, slots))
    three_heads = pltpu.SemaphoreType.DMA((3 * HEAD_COPIES,))
    vec_spec = whole((VECTOR_ROWS, width))
    vec_out = pl.BlockSpec((VECTOR_ROWS, width), lambda *_: (0, 0))

    normed, q, k, v = call(
        functools.partial(project_kernel, heads),
        "project",
        meta,
        [*toks, *squares, vec, cos, sin],
        (heads,),
        [ANYWHERE] * (heads + PIECES) + [vec_spec, table, table],
        [flat] * 4,
        [low] * 4,
        [pair_buffer, square_buffer, square_buffer, square_buffer, row_sems, three_heads],
        cost=(6 * work * width, 8 * work),
    )

    pairs = width // PAIR
    tile = pl.BlockSpec((1, rows, PAIR), lambda n, p, *_: (n, 0, p))

    def attend(meta, slot, before):
        picked = pl.BlockSpec((1, rows, PAIR), lambda p, *_: (slot, 0, p))
        return call(
            functools.partial(attend_kernel, slot),
            "attend",
            meta,
            [q, k, v, *before],
            (pairs,),
            [picked] * 3 + [ANYWHERE] * len(before),
            [picked] * 3,
            [low] * 3,
            cost=(16 * work * rows // slots, 10 * work // slots),
            aliases={4 + i: i for i in range(len(before))},
        )

    attended = []
    now = meta
    for slot in range(slots):
        if slot == 0:
            now, q, block_across = tie(now, q, block_across)
            block_beside = swap(block_across, 1, "seq")
            block_far = swap(block_across, 1)
        elif slot == 1:
            now, block_beside, attended, cots[2] = tie(meta, block_beside, attended, cots[2])
            blocks = [block, block_core, block_across, block_beside, block_far]
            blocks += [swap(block_beside, 1)]
        attended = attend(now, slot, attended)
    context, context_rest, stats = attended

    size = width // PARTS
    o_size = HEADS_EACH * UNIT
    up_shape = jax.ShapeDtypeStruct((2 * PARTS, size, width), BF16)
    down_shape = jax.ShapeDtypeStruct((2 * PARTS, size + o_size, width), BF16)
    ring = heads * (slots * portion // size)
    block_buffer = pltpu.VMEM((heads, width, width), BF16)
    block_sums = pltpu.VMEM((heads, width, width), F32)
    hidden_buffer = pltpu.VMEM((heads, slots * portion, width), BF16)
    row_sums = pltpu.VMEM((slots * portion, width), F32)
    row_buffer = pltpu.VMEM((slots * portion, width), BF16)
    turned_buffer = pltpu.VMEM((width, slots * portion), BF16)
    out = call(
        functools.partial(feed_kernel, heads, (SIDE_ORDER, SEQ_ORDER)),
        "feed",
        meta,
        [*toks, *cots, *squares, *blocks, context, vec, bias_up],
        (heads,),
        [ANYWHERE] * (2 * heads + 2 * PIECES) + [flat, vec_spec, whole((heads, 1, width))],
        [ANYWHERE] * heads + [flat, flat, vec_out] + [ANYWHERE] * 4,
        [piece] * heads + [low, low, vector] + [up_shape] * 2 + [down_shape] * 2,
        [
            pair_buffer,
            pair_buffer,
            pltpu.VMEM((1, slots, portion, width), BF16),
            square_buffer,
            block_buffer,
            block_buffer,
            hidden_buffer,
            hidden_buffer,
            block_sums,
            block_sums,
            pltpu.VMEM((width, width), F32),
            row_sums,
            row_sums,
            row_buffer,
            turned_buffer,
            row_buffer,
            turned_buffer,
            turned_buffer,
            pltpu.VMEM((slots * portion, PAIR), F32),
            row_sems,
            row_sems,
            two,
            pltpu.SemaphoreType.DMA((HEAD_COPIES + 2 * PIECES,)),
            pltpu.SemaphoreType.DMA((ring + 4 * PARTS,)),
        ],
        cost=(54 * work * width, 60 * MIB),
    )
    mixed, out = out[:heads], out[heads:]
    middle_grad, context_grad, feed_vec, up_stay, up_leave, down_stay, down_leave = out


    class Chain:
        def __init__(self, stay, leave, order, back):
            self.state = (stay, leave)
            self.stages = [("half", "core")] + [("half", name) for name in order]
            self.stages += [("full", f"s{bit}") for bit in range(PART_BITS, peer_bits)]
            self.stages += [("back", name) for name in back]
            self.done = 0
            self.first_bits = tuple(int(name[1:]) for name in back)

        @property
        def open(self):
            return self.done < len(self.stages)

        def start(self):
            self.got = move(self.state[1], self.stages[self.done][1])

        def absorb(self):
            kind = self.stages[self.done][0]
            self.done += 1
            if not self.open:
                self.ends = [self.state[0], self.got]
                return
            if kind == "back":
                current = jnp.concatenate([self.state[0], self.got], axis=0)
            else:
                current = add(self.state[0], self.got)
            if self.stages[self.done][0] == "half":
                count = current.shape[0] // 2
                self.state = (current[:count], current[count:])
            else:
                self.state = (current, current)

    class ShortChain:
        def __init__(self, outs, at_once):
            self.state = tuple(outs)
            self.stages = ["head"] if at_once else ["core", "side"]
            self.stages += ["half", "both"]
            self.stages += [f"s{bit}" for bit in range(3, peer_bits)] + ["back"]
            self.done = 0

        @property
        def open(self):
            return self.done < len(self.stages)

        def start(self):
            stage = self.stages[self.done]
            state = self.state
            if stage == "head":
                self.got = tuple(swap(state[k], k) for k in (2, 3, 1))
                self.kept = state[0]
            elif stage == "core":
                self.got = tuple(swap(state[k], 1) for k in (1, 3))
            elif stage == "side":
                self.got = (swap(state[1], 2),)
                self.kept = state[0]
            elif stage == "half":
                self.got = (move(state[1], "s0"),)
                self.kept = state[0]
            elif stage == "both":
                self.got = tuple(swap(state[0], k, "seq") for k in (4, 6, 2))
                self.kept = state[0]
            else:
                self.got = (move(state[0], "s0" if stage == "back" else stage),)
                self.kept = state[0]

        def absorb(self):
            stage = self.stages[self.done]
            self.done += 1
            if stage == "back":
                self.ends = [self.kept, self.got[0]]
                return
            if stage == "core":
                self.state = (add(self.state[0], self.got[0]), add(self.state[2], self.got[1]))
                return
            got = [array.astype(F32) for array in self.got]
            current = self.kept.astype(F32) + got[-1]
            if len(got) == 3:
                current = current + (got[0] + got[1])
            current = current.astype(BF16)
            if self.stages[self.done] == "half":
                self.state = (current[:1], current[1:])
            else:
                self.state = (current,)

    def mark(meta, chains, new=(), extras=()):
        meta, gots, extras = tie(meta, [chain.got for chain in chains], list(extras))
        for chain, got in zip(chains, gots):
            chain.got = got
            chain.absorb()
        active = [chain for chain in chains if chain.open] + list(new)
        meta, states = tie(meta, [chain.state for chain in [*chains, *new]])
        for chain, state in zip([*chains, *new], states):
            chain.state = state
        for chain in active:
            chain.start()
        return meta, active, extras

    up = Chain(up_stay, up_leave, SIDE_ORDER, ("s1", "s0"))
    down = Chain(down_stay, down_leave, SEQ_ORDER, ("s0", "s1"))
    wide_table = whole((rows, PAIR))
    grads = []

    def attend_back(meta, number):
        first, count = CALLS[number]
        shifted = pl.BlockSpec((1, rows, PAIR), lambda n, p, *_: (n, 0, p + first))
        own = pl.BlockSpec((1, rows, PAIR), lambda n, p, *_: (n, 0, p))
        short = jax.ShapeDtypeStruct((slots, rows, count * PAIR), BF16)
        grads.append(
            call(
                attend_back_kernel,
                "attend_back",
                meta,
                [q, k, v, context_grad, context, context_rest, stats, cos, sin],
                (slots, count),
                [shifted] * 7 + [wide_table] * 2,
                [own] * 3 + [pl.BlockSpec((1, 8, PAIR), lambda n, p, *_: (n, 0, p))],
                [short] * 3 + [jax.ShapeDtypeStruct((slots, 8, count * PAIR), F32)],
                [pltpu.VMEM((PAIR, rows), F32)],
                cost=(40 * work * rows * count // pairs, 18 * work * count // pairs),
            )
        )

    def column_spec(array):
        return pl.BlockSpec((slots, portion, array.shape[-1]), lambda k, m: (0, k ^ m[0], 0))

    def weight_chain(meta, parts, head_count, at_once):
        arrays = [array for part in parts for array in part[:3]]
        shape = (2, 3 * head_count * HD // 2, width)
        outs = call(
            functools.partial(weight_kernel, len(parts), head_count),
            "weight_back",
            meta,
            [*arrays, normed],
            (heads,),
            [column_spec(array) for array in arrays] + [flat],
            [pl.BlockSpec(shape, lambda *_: (0, 0, 0))] * heads,
            [jax.ShapeDtypeStruct(shape, BF16)] * heads,
            [pltpu.VMEM((3 * head_count * heads * HD, width), F32)],
            cost=(2 * work * head_count * heads * HD * 3, 8 * work),
        )
        return ShortChain(outs, at_once)

    def placed(meta, moved, name):
        shape = (slots, heads, portion, width)
        return call(
            functools.partial(place_kernel, heads),
            name,
            meta,
            moved,
            (1,),
            [whole((slots, portion, width))] * heads,
            whole(shape),
            jax.ShapeDtypeStruct(shape, BF16),
            cost=(0, 4 * work),
        ).reshape(total_slots, portion, width)

    now, active, _ = mark(meta, [], [up, down])
    attend_back(now, 0)
    now, active, _ = mark(tie(meta, grads[0])[0], active)
    attend_back(now, 1)
    now, active, _ = mark(tie(meta, grads[1])[0], active)
    now, mixed_two, mixed_three = tie(now, mixed[2], mixed[3])
    mixed_two, mixed_three = swap(mixed_two, 2), swap(mixed_three, 3)
    attend_back(now, 2)
    early = weight_chain(now, grads[:3], 2, False)
    now, active, _ = mark(tie(meta, grads[2], early.state)[0], active, [early])
    attend_back(now, 3)
    now, active, _ = mark(tie(meta, grads[3])[0], active)
    attend_back(now, 4)
    late = weight_chain(now, grads[3:], 1, True)
    now, active, (mixed_two, mixed_three) = mark(
        tie(meta, late.state)[0], active, [late], [mixed_two, mixed_three]
    )
    mixed_moved = [mixed[0], swap(mixed[1], 1), mixed_two, mixed_three]

    own_codons = lax.dynamic_index_in_dim(
        codons.reshape(slots, heads, rows), here, 1, keepdims=False
    )
    own_owners = lax.dynamic_index_in_dim(
        owners.reshape(slots, heads), here, 1, keepdims=False
    )
    live = jnp.arange(rows)[None, :] < own_lengths[:, None]
    matches = (own_codons[:, :, None] == jnp.arange(CODONS)[None, None, :]) & live[:, :, None]
    counts = jnp.sum(matches.astype(F32), axis=1)
    owned = (own_owners[None, :] == jnp.arange(peers)[:, None]).astype(F32)
    counts = jnp.sum(owned[:, :, None] * counts[None, :, :], axis=1).reshape(-1)
    free = (VECTOR_ROWS - named - heads) * width
    counts = jnp.pad(counts, (0, free - counts.shape[0])).reshape(-1, width)
    vec_in = jnp.concatenate([feed_vec[: named + heads], counts], axis=0)

    columns = len(CALLS)

    def input_back(meta, first, number, vec_in):
        chosen = pl.BlockSpec((slots, portion, width), lambda k, m: (0, (k + first) ^ m[0], 0))
        specs = []
        for part in grads:
            specs += [
                pl.BlockSpec(
                    (slots, portion, array.shape[-1]), lambda k, m: (0, (k + first) ^ m[0], 0)
                )
                for array in part[:3]
            ]
            specs += [whole(part[3].shape)]
        out = call(
            functools.partial(input_kernel, number, columns, True),
            "input_back",
            meta,
            [
                *toks[first : first + number],
                *squares,
                *[array for part in grads for array in part],
                vec,
                vec_in,
                middle_grad,
            ],
            (number,),
            [ANYWHERE] * (number + PIECES) + specs + [vec_spec, vec_spec, chosen],
            [ANYWHERE] * number + [vec_out],
            [piece] * number + [vector],
            [
                pair_buffer,
                pair_buffer,
                square_buffer,
                square_buffer,
                square_buffer,
                row_sems,
                two,
                three_heads,
            ],
            cost=(6 * work * width * number // heads, 16 * work * number // heads),
        )
        return out[:number], out[number]

    pieces, all_vec = input_back(now, 0, heads, vec_in)
    now, active, _ = mark(tie(meta, all_vec)[0], active)
    now, all_vec, pieces = tie(now, all_vec, pieces)
    piece_three, piece_two = swap(pieces[3], 3), swap(pieces[2], 2)
    piece_own, piece_core = pieces[0], swap(pieces[1], 1)
    one_vec = swap(all_vec, 1, "seq")
    mixed_out = placed(now, mixed_moved, "place_mixed")
    now, active, (piece_three, piece_two, one_vec, mixed_out) = mark(
        now, active, extras=[piece_three, piece_two, one_vec, mixed_out]
    )
    while up.open or down.open:
        now, active, _ = mark(now, active)
    all_vec = all_vec + one_vec
    seq_vec = [swap(all_vec, k, "seq") for k in (4, 6, 2)]
    input_out = placed(now, [piece_own, piece_core, piece_two, piece_three], "place_input")
    grad_up = call(
        functools.partial(unpack_up_kernel, up.first_bits),
        "unpack_up",
        now,
        up.ends,
        (1,),
        [whole(array.shape) for array in up.ends],
        whole((width, width)),
        jax.ShapeDtypeStruct((width, width), F32),
        cost=(0, 6 * width * width),
    )
    now, active, (*seq_vec, input_out, grad_up) = mark(
        now, active, extras=[*seq_vec, input_out, grad_up]
    )
    all_vec = (all_vec + seq_vec[2]) + (seq_vec[0] + seq_vec[1])
    for bit in range(3, peer_bits):
        all_vec = all_vec + swap(all_vec, 1 << bit, "seq")
    own_vec = [swap(all_vec, k) for k in (2, 3, 1)]
    grad_down, grad_out = call(
        functools.partial(unpack_down_kernel, down.first_bits),
        "unpack_down",
        now,
        down.ends,
        (1,),
        [whole(array.shape) for array in down.ends],
        [whole((width, width)), whole((part_width, width))],
        [
            jax.ShapeDtypeStruct((width, width), F32),
            jax.ShapeDtypeStruct((part_width, width), F32),
        ],
        [pltpu.VMEM((width, width), F32)],
        cost=(0, 8 * width * width),
    )
    while active:
        now, active, _ = mark(now, active)
    own_vec, grad_down = tie(own_vec, grad_down)
    all_vec = (all_vec + own_vec[2]) + (own_vec[0] + own_vec[1])

    def half_spec(array):
        return whole(array.shape)

    head_shape = jax.ShapeDtypeStruct((part_width, width), F32)
    sources = [*early.ends, *late.ends]
    grad_q, grad_k, grad_v = call(
        functools.partial(unpack_heads_kernel, 2),
        "unpack_heads",
        meta,
        sources,
        (1,),
        [half_spec(array) for array in sources],
        [whole((part_width, width))] * 3,
        [head_shape] * 3,
        cost=(0, 6 * width * width),
    )

    by_head = lax.dynamic_index_in_dim(
        all_vec[:3].reshape(3, HEADS_EACH, heads, HD), here, 2, keepdims=False
    ).reshape(3, part_width)
    sums = lax.dynamic_slice_in_dim(all_vec[3:named], here * part_width, part_width, 1)
    dbq, dbk, dbv = [by_head[i] for i in range(3)]
    dbo, dbd, dg1, db1, dg2, db2 = [sums[i] for i in range(named - 3)]
    grad_b_up = lax.dynamic_index_in_dim(all_vec[named:], here, 0, keepdims=False)
    histogram = lax.dynamic_slice_in_dim(
        all_vec[named + heads :].reshape(1, -1), position * CODONS, CODONS, 1
    ).astype(jnp.int32)
    return (
        mixed_out,
        input_out,
        dg1,
        db1,
        grad_q,
        dbq,
        grad_k,
        dbk,
        grad_v,
        dbv,
        grad_out,
        dbo,
        dg2,
        db2,
        grad_up,
        grad_b_up,
        grad_down,
        dbd,
        histogram,
    )


def solution(mesh):
    return jax.shard_map(
        local,
        mesh=mesh,
        in_specs=(
            P("seq", "head", None),
            P("seq", "head", None),
            P("seq"),
            P("seq"),
            P("seq", None),
            P("head"),
            P("head"),
            P("head", None),
            P("head"),
            P("head", None),
            P("head"),
            P("head", None),
            P("head"),
            P("head", None),
            P("head"),
            P("head"),
            P("head"),
            P(None, "head"),
            P("head"),
            P("head", None),
            P("head"),
        ),
        out_specs=(
            P("seq", "head", None),
            P("seq", "head", None),
            P("head"),
            P("head"),
            P("head", None),
            P("head"),
            P("head", None),
            P("head"),
            P("head", None),
            P("head"),
            P("head", None),
            P("head"),
            P("head"),
            P("head"),
            P(None, "head"),
            P("head"),
            P("head", None),
            P("head"),
            P("seq", None),
        ),
        check_vma=False,
    )
```
